32 devices in a mesh: grp: 4 (over z), sub: 8 (over y, x, core).
Axes of the slice: x: 2, y: 2, z: 4, core: 2. Of those that a mesh axis runs over, the one named last changes fastest.
Arguments:
- jump_data: float32 [4, 8, 256, 512], P('grp', 'sub'), as said below
- dual_block: float32 [4, 8, 512, 512], P('grp', 'sub'), as said below
- dirichlet_block: float32 [4, 8, 512, 512], P('grp', 'sub'), as said below
- coupling: float32 [4, 8, 512, 24], P('grp', 'sub'), may hold values from -0.25 to 0.25
- corner_weight: float32 [4, 8, 24], P('grp', 'sub'), may hold values from 0.2 to 2
- corner_rows: int32 [4, 8, 24], P('grp', 'sub'), may hold values from 0 to 47
- membership: int32 [4, 8], P('grp', 'sub'), may hold values from 0 to 3
- face_pairing: int32 [4, 8, 2, 128], P('grp', 'sub'), may hold values from 0 to 127, each once within a row
- block_pattern: int32 [4, 8, 4, 4], P('grp', 'sub'), may hold values from 0 to 1, as said below
Outputs:
- solution: float32 [4, 8, 256, 512], P('grp', 'sub')
- residual: float32 [4, 8, 256, 512], P('grp', 'sub')
The draws below stay inside these ranges and needn't reach their ends.
Inputs may be any that keep to these rules, and one draw needn't show every extreme that they name: `jump_data`: the scale of one load case's data tends to grow from the first device to the last. `dual_block`: symmetric and positive definite. `dirichlet_block`: symmetric and positive definite. `block_pattern`: symmetric 0/1 masks with ones on the diagonal; the number of kept blocks differs between subdomains. `corner_rows`: corner rows of a subdomain may repeat across subdomains of the same cluster. `membership`: cluster sizes differ within a group. `face_pairing`: each row is a permutation of 0 to 127.
All inputs are finite; a program needn't handle non-finite values.
Results may differ from the reference program's by a relative error of at most 0.0003.
Values sent between devices are 32-bit elements; how exact they have to be, the bound alone decides.
No kernel may reach another device: no remote copies, remote signals or barrier semaphores. Data moves between devices by JAX's collectives and lax.ppermute only.
A program may use at most 64 MiB of HBM per device.

```python
import math
import jax
import jax.numpy as jnp
from jax import lax

FACE = 128
LOADS = 512
NC = 24
NCG = 48
NCLUST = 4
ITERS = 2
NI = 512
NL = 256
GROUPS = 4
MEMBERS = 8


def stiffness_levels(key):
    return jnp.exp(jax.random.uniform(key, (GROUPS, MEMBERS, 1, 1), jnp.float32, 0.0, math.log(10.0)))


def symmetric_block(key, low, high):
    first_key, second_key = jax.random.split(key)
    spread = jax.random.uniform(first_key, (GROUPS, MEMBERS, NI, NI), jnp.float32, -2.0, 2.0) / math.sqrt(NI)
    spread = 0.5 * (spread + jnp.swapaxes(spread, -1, -2))
    diagonal = jax.random.uniform(second_key, (GROUPS, MEMBERS, 1, NI), jnp.float32, low, high)
    identity = jnp.eye(NI, dtype=jnp.float32)
    return spread * (1.0 - identity) + identity * diagonal


def draw_dual_block(key, part):
    levels = stiffness_levels(key)
    key = jax.random.fold_in(key, 2)
    return symmetric_block(key, 2.5, 4.0) / levels


def draw_dirichlet_block(key, part):
    levels = stiffness_levels(key)
    key = jax.random.fold_in(key, 3)
    return symmetric_block(key, 2.5, 4.0) * levels


def draw_jump_data(key, part):
    key = jax.random.fold_in(key, 5)
    base_key, column_key = jax.random.split(key, 2)
    position = jnp.arange(GROUPS * MEMBERS, dtype=jnp.float32).reshape(GROUPS, MEMBERS, 1, 1)
    device_scale = 3.0 ** (position / max(GROUPS * MEMBERS - 1, 1))
    column_scale = jnp.exp(jax.random.uniform(column_key, (1, 1, 1, LOADS), jnp.float32, math.log(0.3), math.log(3.0)))
    values = jnp.clip(jax.random.normal(base_key, (GROUPS, MEMBERS, NL, LOADS), jnp.float32), -4.0, 4.0)
    return values * device_scale * column_scale


def draw_block_pattern(key, part):
    key = jax.random.fold_in(key, 7)
    density_key, bits_key = jax.random.split(key)
    density = jax.random.randint(density_key, (GROUPS, MEMBERS, 1, 1), 0, 9)
    bits = (jax.random.randint(bits_key, (GROUPS, MEMBERS, 4, 4), 0, 10) <= density).astype(jnp.int32)
    upper = jnp.triu(bits, 1)
    pattern = upper + jnp.swapaxes(upper, -1, -2) + jnp.eye(4, dtype=jnp.int32)
    return jnp.minimum(pattern, 1).astype(jnp.int32)


def plant(array, stream_key, smallest, high):
    shape = array.shape
    spot = [jax.random.randint(jax.random.fold_in(stream_key, axis), (), 0, shape[axis]) for axis in range(len(shape))]
    array = array.at[tuple(spot)].set(smallest)
    longest = shape.index(max(shape))
    spot[longest] = (spot[longest] + 1) % shape[longest]
    return array.at[tuple(spot)].set(high)


def block_levels(key, shape, cuts, low, high):
    loudness = 1.0
    for dim, parts in cuts:
        steps = jax.random.uniform(jax.random.fold_in(jax.random.fold_in(key, 6), dim), (parts,), jnp.float32, low / len(cuts), high / len(cuts))
        loudness = loudness * jnp.repeat(jnp.exp(steps), shape[dim] // parts).reshape((-1,) + (1,) * (len(shape) - 1 - dim))
    return loudness


def gaussian(own_key, shape, deviation, bound, cuts=(), kind=jnp.bfloat16):
    array = deviation * jax.random.normal(own_key, shape, jnp.float32)
    if cuts:
        array = array * block_levels(own_key, shape, cuts, -0.22, 0.18)
    return jnp.clip(array, -bound, bound).astype(kind)


def setup_inputs(seed: int = 0) -> dict:
    streams_of = jax.random.split(jax.random.key(seed), 10)
    jump_data = draw_jump_data(jax.random.fold_in(streams_of[9], 71), 0)
    dual_block = draw_dual_block(jax.random.fold_in(streams_of[9], 71), 0)
    dirichlet_block = draw_dirichlet_block(jax.random.fold_in(streams_of[9], 71), 0)
    coupling = gaussian(streams_of[3], (GROUPS, MEMBERS, NI, NC), NI ** -0.5, 0.25, ((0, 4), (1, 8)), jnp.float32)
    corner_weight = jnp.clip(jnp.exp(math.log(2.0) - 2.3025851 * jax.random.uniform(streams_of[4], (GROUPS, MEMBERS, NC), jnp.float32) ** block_levels(streams_of[4], (GROUPS, MEMBERS, NC), ((0, 4), (1, 8)), -0.2, 0.2)), 0.2, 2.0)
    corner_rows = plant(jax.random.randint(streams_of[5], (GROUPS, MEMBERS, NC), 0, NCG), jax.random.fold_in(streams_of[5], 1), 0, NCG - 1).astype(jnp.int32)
    membership = plant(jax.random.randint(streams_of[6], (GROUPS, MEMBERS), 0, NCLUST), jax.random.fold_in(streams_of[6], 1), 0, NCLUST - 1).astype(jnp.int32)
    face_pairing = jax.vmap(lambda own: jax.random.permutation(own, FACE))(jax.random.split(streams_of[7], GROUPS * MEMBERS * 2)).reshape((GROUPS, MEMBERS, 2, FACE)).astype(jnp.int32)
    block_pattern = draw_block_pattern(jax.random.fold_in(streams_of[9], 71), 0)
    return {"jump_data": jump_data, "dual_block": dual_block, "dirichlet_block": dirichlet_block, "coupling": coupling, "corner_weight": corner_weight, "corner_rows": corner_rows, "membership": membership, "face_pairing": face_pairing, "block_pattern": block_pattern}


highest = lax.Precision.HIGHEST


def pair_tables(face_pairing):
    return (face_pairing[..., :, None] == jnp.arange(FACE, dtype=jnp.int32)).astype(jnp.float32)


def spread_field(multipliers, tables):
    right_part = multipliers[:, :, :FACE]
    upper_part = multipliers[:, :, FACE:]
    from_left = jnp.roll(right_part, 1, axis=1)
    from_below = jnp.roll(upper_part, 1, axis=0)
    left_face = -jnp.einsum("gsji,gsir->gsjr", tables[:, :, 0], from_left, precision=highest)
    lower_face = -jnp.einsum("gsji,gsir->gsjr", tables[:, :, 1], from_below, precision=highest)
    return jnp.concatenate([right_part, left_face, upper_part, lower_face], axis=2)


def collect_field(local, tables):
    send_left = jnp.einsum("gsji,gsjr->gsir", tables[:, :, 0], local[:, :, FACE:2 * FACE], precision=highest)
    send_down = jnp.einsum("gsji,gsjr->gsir", tables[:, :, 1], local[:, :, 3 * FACE:], precision=highest)
    first_rows = local[:, :, :FACE] - jnp.roll(send_left, -1, axis=1)
    second_rows = local[:, :, 2 * FACE:3 * FACE] - jnp.roll(send_down, -1, axis=0)
    return jnp.concatenate([first_rows, second_rows], axis=2)


def reference(jump_data, dual_block, dirichlet_block, coupling, corner_weight, corner_rows, membership, face_pairing, block_pattern):
    tables = pair_tables(face_pairing)
    block_mask = jnp.repeat(jnp.repeat(block_pattern, FACE, axis=2), FACE, axis=3).astype(jnp.float32)
    dual_masked = dual_block * block_mask
    dirichlet_masked = dirichlet_block * block_mask
    same_cluster = (membership[:, :, None] == membership[:, None, :]).astype(jnp.float32)
    same_row = (corner_rows[:, :, :, None, None] == corner_rows[:, None, None, :, :]).astype(jnp.float32)
    link_table = same_row * same_cluster[:, :, None, :, None]
    denominator = jnp.einsum("gsjmi,gmi->gsj", link_table, corner_weight, precision=highest)[..., None]

    def dual_apply(multipliers):
        spread = spread_field(multipliers, tables)
        local = jnp.einsum("gsab,gsbr->gsar", dual_masked, spread, precision=highest)
        corners = jnp.einsum("gsac,gsar->gscr", coupling, spread, precision=highest)
        coarse = jnp.einsum("gsjmi,gmir->gsjr", link_table, corners, precision=highest) / denominator
        local = local + jnp.einsum("gsac,gscr->gsar", coupling, coarse, precision=highest)
        return collect_field(local, tables)

    def precondition(multipliers):
        spread = spread_field(multipliers, tables)
        return collect_field(jnp.einsum("gsab,gsbr->gsar", dirichlet_masked, spread, precision=highest), tables)

    def inner(first, second):
        return jnp.sum(first * second, axis=(0, 1, 2))

    solution = jnp.zeros_like(jump_data)
    residual = jump_data
    search = precondition(residual)
    direction = search
    gamma = inner(residual, search)
    for iteration in range(ITERS):
        image = dual_apply(direction)
        alpha = gamma / inner(direction, image)
        solution = solution + alpha * direction
        residual = residual - alpha * image
        if iteration + 1 < ITERS:
            search = precondition(residual)
            gamma_next = inner(residual, search)
            direction = search + (gamma_next / gamma) * direction
            gamma = gamma_next
    return solution, residual
```

```python
import jax
import jax.numpy as jnp
from jax import lax
from jax.sharding import PartitionSpec as P

ITERS = 2

high = lax.Precision.HIGH
highest = lax.Precision.HIGHEST


def matmul(first, second, precision=high):
    return jnp.dot(first, second, precision=precision, preferred_element_type=jnp.float32)


def move(array, axis, target):
    peers = lax.axis_size(axis)
    return lax.ppermute(array, axis, [(i, target(i) % peers) for i in range(peers)])


def near(i):
    return i ^ 1


def far(i):
    return i - 1 if i % 2 == 0 else i + 1


def swap_edges(parts):
    return (
        move(parts[0], "sub", near),
        move(parts[1], "sub", far),
        move(parts[2], "grp", near),
        move(parts[3], "grp", far),
    )


def gather_members(array):
    peers = lax.axis_size("sub")
    same = [array] + [move(array, "sub", lambda i, k=k: i ^ k) for k in range(2, peers, 2)]
    same = jnp.concatenate(same, axis=0)
    return jnp.concatenate([same, move(same, "sub", near)], axis=0)


def sum_everywhere(array):
    for axis in ("sub", "grp"):
        step = 1
        while step < lax.axis_size(axis):
            array = array + move(array, axis, lambda i, k=step: i ^ k)
            step *= 2
    return array


def column_sum(first, second):
    return jnp.sum(first * second, axis=0)


def per_device(
    jump_data,
    dual_block,
    dirichlet_block,
    coupling,
    corner_weight,
    corner_rows,
    membership,
    face_pairing,
    block_pattern,
):
    face = face_pairing.shape[-1]
    corners = corner_rows.shape[-1]
    pattern = block_pattern[0, 0]
    odd_sub = lax.axis_index("sub") % 2 == 1
    odd_grp = lax.axis_index("grp") % 2 == 1

    identity = jnp.eye(face, dtype=jnp.float32)
    nothing = jnp.zeros((face, face), jnp.float32)

    def pair_table(pairing):
        return (pairing[:, None] == jnp.arange(face, dtype=jnp.int32)[None, :]).astype(jnp.float32)

    def turn(pairing, odd):
        table = -pair_table(pairing)
        first = jnp.concatenate([jnp.where(odd, nothing, identity), jnp.where(odd, identity, nothing)], 1)
        second = jnp.concatenate([jnp.where(odd, table, nothing), jnp.where(odd, nothing, table)], 1)
        return jnp.concatenate([first, second], 0)

    turn_sub = turn(face_pairing[0, 0, 0], odd_sub)
    turn_grp = turn(face_pairing[0, 0, 1], odd_grp)
    blank = jnp.zeros_like(turn_sub)
    turning = jnp.concatenate(
        [jnp.concatenate([turn_sub, blank], 1), jnp.concatenate([blank, turn_grp], 1)], 0
    )

    jump = jump_data[0, 0]
    right, upper = jump[:face], jump[face:]
    from_left = move(right, "sub", lambda i: i + 1)
    from_below = move(upper, "grp", lambda i: i + 1)

    block_mask = jnp.repeat(jnp.repeat(pattern, face, axis=0), face, axis=1).astype(jnp.float32)

    def turned(block):
        return matmul(turning.T, matmul(block * block_mask, turning))

    dirichlet_local = turned(dirichlet_block[0, 0])
    dual_local = turned(dual_block[0, 0])
    coupling_local = matmul(turning.T, coupling[0, 0])

    label = jnp.concatenate(
        [
            corner_weight[0, 0],
            corner_rows[0, 0].astype(jnp.float32),
            jnp.broadcast_to(membership[0, 0].astype(jnp.float32), (corners,)),
        ]
    ).reshape(1, 3, corners)
    labels = gather_members(label)
    weights_every, rows_every, members_every = (labels[:, i].reshape(-1) for i in range(3))
    link_table = (
        (rows_every[None, :] == rows_every[:corners, None])
        & (members_every[None, :] == members_every[:corners, None])
    ).astype(jnp.float32)
    denominator = matmul(link_table, weights_every[:, None], highest)
    coarse_table = matmul(coupling_local, link_table / denominator)

    def slots(array):
        return tuple(array[i * face : (i + 1) * face] for i in range(4))

    def assemble(local):
        return jnp.concatenate([a + b for a, b in zip(slots(local), swap_edges(slots(local)))], 0)

    def dual_apply(field):
        every = gather_members(matmul(coupling_local.T, field))
        return matmul(dual_local, field) + matmul(coarse_table, every)

    residual = jnp.concatenate(
        [
            jnp.where(odd_sub, from_left, right),
            jnp.where(odd_sub, right, from_left),
            jnp.where(odd_grp, from_below, upper),
            jnp.where(odd_grp, upper, from_below),
        ],
        0,
    )
    search_local = matmul(dirichlet_local, residual)
    gamma_part = column_sum(residual, search_local)
    search = assemble(search_local)
    image_local = dual_apply(search)
    sums = sum_everywhere(jnp.stack([gamma_part, column_sum(search, image_local)]))
    gamma, alpha = sums[0], sums[0] / sums[1]
    image = assemble(image_local)

    later = assemble(matmul(dirichlet_local, image))
    residual_next = residual - alpha * image
    search_next = search - alpha * later
    later_local = dual_apply(search_next)
    parts = jnp.stack(
        [
            0.5 * column_sum(residual_next, search_next),
            column_sum(search_next, later_local),
            0.5 * column_sum(search_next, image),
            column_sum(search, later_local),
        ]
    )
    gamma_next, steep, cross, cross_other = sum_everywhere(parts)
    beta = gamma_next / gamma
    alpha_next = gamma_next / (steep + beta * (cross + cross_other + beta * sums[1]))

    def owned(array):
        a, b, c, d = slots(array)
        return jnp.concatenate([jnp.where(odd_sub, b, a), jnp.where(odd_grp, d, c)], 0)

    a, b, c, d = slots(later_local)
    back = jnp.concatenate(
        [
            move(jnp.where(odd_sub, a, b), "sub", lambda i: i - 1),
            move(jnp.where(odd_grp, c, d), "grp", lambda i: i - 1),
        ],
        0,
    )
    later_image = owned(later_local) + back
    search_own = owned(search)
    solution = alpha * search_own + alpha_next * (owned(search_next) + beta * search_own)
    final = owned(residual_next) - alpha_next * (later_image + beta * owned(image))
    return (solution[None, None], final[None, None])


def solution(mesh):
    placed = (
        P("grp", "sub", None, None),
        P("grp", "sub", None, None),
        P("grp", "sub", None, None),
        P("grp", "sub", None, None),
        P("grp", "sub", None),
        P("grp", "sub", None),
        P("grp", "sub"),
        P("grp", "sub", None, None),
        P("grp", "sub", None, None),
    )
    return jax.shard_map(
        per_device,
        mesh=mesh,
        in_specs=placed,
        out_specs=(P("grp", "sub", None, None), P("grp", "sub", None, None)),
        check_vma=False,
    )
```

```python
import functools

import jax
import jax.numpy as jnp
from jax import lax
from jax.experimental import pallas as pl
from jax.experimental.pallas import tpu as pltpu
from jax.sharding import PartitionSpec as P

ITERS = 2
CHUNKS = 1
LIMIT = 8 * 1024 * 1024

VMEM = pl.BlockSpec(memory_space=pltpu.VMEM)
SMEM = pl.BlockSpec(memory_space=pltpu.SMEM)
wide = jnp.float32
short = jnp.bfloat16
highest = lax.Precision.HIGHEST


def call(body, inputs, outputs, scratch=(), flops=0, scalars=1):
    moved = sum(x.size * x.dtype.itemsize for x in inputs)
    return pl.pallas_call(
        body,
        out_shape=[jax.ShapeDtypeStruct(shape, kind) for shape, kind in outputs],
        in_specs=[SMEM] * scalars + [VMEM] * (len(inputs) - scalars),
        out_specs=[VMEM] * len(outputs),
        scratch_shapes=[pltpu.VMEM(shape, kind) for shape, kind in scratch],
        compiler_params=pltpu.CompilerParams(vmem_limit_bytes=LIMIT),
        cost_estimate=pl.CostEstimate(flops=flops, bytes_accessed=moved, transcendentals=0),
    )(*inputs)


def move(array, axis, target):
    peers = lax.axis_size(axis)
    return lax.ppermute(array, axis, [(i, target(i) % peers) for i in range(peers)])


def near(i):
    return i ^ 1


def far(i):
    return i - 1 if i % 2 == 0 else i + 1


def swap_edges(parts):
    last = move(parts[3], "grp", far)
    return [
        move(parts[0], "sub", near),
        move(parts[1], "sub", far),
        move(parts[2], "grp", near),
        last,
    ]


def gather_members(array):
    peers = lax.axis_size("sub")
    same = [array] + [move(array, "sub", lambda i, k=k: i ^ k) for k in range(2, peers, 2)]
    return same + [move(one, "sub", near) for one in same]


def group_terms(array):
    peers = lax.axis_size("grp")
    if peers <= 4:
        return [array] + [move(array, "grp", lambda i, k=k: i + k) for k in range(1, peers)]
    step = 1
    while step < peers:
        array = array + move(array, "grp", lambda i, k=step: i ^ k)
        step *= 2
    return [array]


def dot(first, second, precision=None):
    return jnp.dot(first, second, precision=precision, preferred_element_type=wide)


def dot_across(first, second):
    return lax.dot_general(first, second, (((1,), (1,)), ((), ())), preferred_element_type=wide)


def halves(value):
    high = value.astype(short)
    return high, (value - high.astype(wide)).astype(short)


def put_triple(ref, rows, value):
    depth = ref.shape[0] // 3
    high, low = halves(value)
    ref[pl.ds(rows, value.shape[0])] = high
    ref[pl.ds(depth + rows, value.shape[0])] = low
    ref[pl.ds(2 * depth + rows, value.shape[0])] = high


def column_sum(first, second):
    return jnp.sum(first * second, axis=0, keepdims=True)


def turning(odd, pairing):
    face = pairing.shape[-1]
    place = lax.broadcasted_iota(jnp.int32, (face, face), 0)
    table = jnp.where(place == pairing, -1.0, 0.0)
    identity = jnp.where(place == lax.broadcasted_iota(jnp.int32, (face, face), 1), 1.0, 0.0)
    chosen = jnp.where(odd == 1, 1.0, 0.0)
    top = jnp.concatenate([identity * (1.0 - chosen), table * chosen], 1)
    bottom = jnp.concatenate([identity * chosen, table * (1.0 - chosen)], 1)
    return jnp.concatenate([top, bottom], 0).astype(short)


def turn_block(odd, pattern, block, pairing, out):
    face = pairing.shape[-1]
    pair = 2 * face
    depth = 2 * pair
    turns = [turning(odd[a], pairing[a : a + 1]) for a in range(2)]
    for a in range(2):
        for b in range(2):
            rows = []
            for i in range(2):
                rows.append(
                    jnp.concatenate(
                        [
                            block[
                                pl.ds((2 * a + i) * face, face), pl.ds((2 * b + j) * face, face)
                            ]
                            * pattern[2 * a + i, 2 * b + j].astype(wide)
                            for j in range(2)
                        ],
                        1,
                    )
                )
            for k, part in enumerate(halves(jnp.concatenate(rows, 0))):
                part = dot_across(dot(turns[a], part).astype(short), turns[b]).astype(short)
                here = pl.ds(a * pair, pair)
                if k == 0:
                    out[here, pl.ds(b * pair, pair)] = part
                    out[here, pl.ds(depth + b * pair, pair)] = part
                else:
                    out[here, pl.ds(2 * depth + b * pair, pair)] = part
    return turns


def dirichlet_kernel(odd, pattern, block, pairing, out):
    turn_block(odd, pattern, block, pairing, out)


def dual_kernel(odd, pattern, block, pairing, coupling, out, table, flat):
    turns = turn_block(odd, pattern, block, pairing, out)
    pair = 2 * pairing.shape[-1]
    depth = 2 * pair
    for a in range(2):
        here = pl.ds(a * pair, pair)
        high, low = (dot_across(v, turns[a]) for v in halves(coupling[:, here]))
        table[here] = (high + low).T
        flat[:, here] = high.astype(short)
        flat[:, pl.ds(depth + a * pair, pair)] = high.astype(short)
        flat[:, pl.ds(2 * depth + a * pair, pair)] = low.astype(short)


def label_kernel(member, weight, rows, out):
    corners = rows.shape[-1]
    out[...] = jnp.full(out.shape, -1.0, wide)
    out[:1, :corners] = weight[...]
    out[1:2, :corners] = rows[...].astype(wide)
    out[2:3, :corners] = jnp.full((1, corners), member[0, 0].astype(wide))


def table_kernel(coupling, *refs):
    labels, (apply, table, columns) = refs[:-3], refs[-3:]
    corners = coupling.shape[1]
    rows = corners + 8
    columns[...] = jnp.zeros(columns.shape, wide)
    for i, label in enumerate(labels):
        columns[pl.ds(i * rows, rows), :8] = label[...].T[:rows]
    across = columns[...].T
    weight, row, member = (across[i : i + 1] for i in range(3))
    same = (columns[:, 1:2] == row) & (columns[:, 2:3] == member) & (columns[:, 1:2] >= 0)
    linked = jnp.where(same, 1.0, 0.0)
    total = jnp.sum(linked * weight, axis=1, keepdims=True)
    table[...] = linked / jnp.where(total > 0, total, 1.0)
    high, low = halves(dot(coupling[...], table[:corners], highest))
    width = table.shape[1]
    apply[:, :width] = high
    apply[:, width : 2 * width] = high
    apply[:, 2 * width :] = low


def start_kernel(odd, matrix, right, upper, from_left, from_below, field, triple, last):
    face = from_left.shape[0]
    for axis, (own, other) in enumerate(((right, from_left), (upper, from_below))):
        here = pl.ds(2 * axis * face, face)
        there = pl.ds((2 * axis + 1) * face, face)
        first = jnp.where(odd[axis] == 1, other[...], own[...])
        second = jnp.where(odd[axis] == 1, own[...], other[...])
        field[here] = first
        field[there] = second
        put_triple(triple, 2 * axis * face, first)
        put_triple(triple, (2 * axis + 1) * face, second)
    last[...] = dot(matrix[pl.ds(3 * face, face)], triple[...])


def start_rest_kernel(matrix, triple, field, last, first, second, third, sums):
    face = last.shape[0]
    total = column_sum(field[pl.ds(3 * face, face)], last[...])
    local = dot(matrix[: 3 * face], triple[...])
    for i, out in enumerate((first, second, third)):
        out[...] = local[i * face : (i + 1) * face]
    sums[...] = jnp.broadcast_to(total + column_sum(field[: 3 * face], local), sums.shape)


def dual_first_kernel(matrix, flat, gamma, *refs):
    parts, others, (field, dense, message, triple) = refs[:4], refs[7:3:-1], refs[8:]
    face = parts[0].shape[0]
    corners = flat.shape[0]
    for i in range(4):
        value = parts[i][...] + others[i][...]
        field[pl.ds(i * face, face)] = value
        put_triple(triple, i * face, value)
    local = dot(matrix[...], triple[...])
    dense[...] = local
    message[:corners] = dot(flat[...], triple[...])
    message[pl.ds(corners, 8)] = jnp.zeros((8, field.shape[1]), wide)
    message[pl.ds(corners, 1)] = gamma[:1]
    message[pl.ds(corners + 1, 1)] = column_sum(field[...], local)


def coarse_last_kernel(table, dense, *refs):
    every, (triple, last) = refs[:-2], refs[-2:]
    face = last.shape[0]
    for i, message in enumerate(every):
        put_triple(triple, i * message.shape[0], message[...])
    last[...] = dense[pl.ds(3 * face, face)] + dot(table[pl.ds(3 * face, face)], triple[...])


def plane_sums(every, sizes, table, values, total):
    rows = every[0].shape[0]
    for i, message in enumerate(every):
        values[pl.ds(i * rows, rows)] = message[...]
    coarse = dot(table[...], values[...], highest)
    sums = every[0][pl.ds(rows - 8, 8)]
    for message in every[1:]:
        sums = sums + message[pl.ds(rows - 8, 8)]
    total[...] = sums
    for place, group in sizes:
        extra = jnp.zeros((1, total.shape[1]), wide)
        for i, message in enumerate(group):
            here = slice(i * rows, i * rows + rows - 8)
            extra = extra + column_sum(coarse[here], message[pl.ds(0, rows - 8)])
        total[pl.ds(place, 1)] = sums[place : place + 1] + extra


def coarse_rest_kernel(table, dense, triple, coarse_table, *refs):
    every, (first, second, third, total, values) = refs[:-5], refs[-5:]
    face = first.shape[0]
    local = dense[: 3 * face] + dot(table[: 3 * face], triple[...])
    first[...] = local[:face]
    second[...] = local[face : 2 * face]
    plane_sums(every, [(1, every)], coarse_table, values, total)
    third[:face] = local[2 * face :]
    third[pl.ds(face, 8)] = total[...]


def energy_kernel(count, table, *refs):
    total, values = refs[-2:]
    plane_sums(refs[:count], [(2, refs[:count]), (3, refs[count:-2])], table, values, total)


def second_last_kernel(matrix, total, *refs):
    parts, others, (field, triple, last) = refs[:4], refs[7:3:-1], refs[8:]
    face = parts[0].shape[0]
    for i in range(4):
        value = parts[i][:face] + others[i][:face]
        field[pl.ds(i * face, face)] = value
        put_triple(triple, i * face, value)
    last[:face] = dot(matrix[pl.ds(3 * face, face)], triple[...])
    last[pl.ds(face, 8)] = total[...] + others[2][pl.ds(face, 8)]


def second_rest_kernel(matrix, triple, *outs):
    face = outs[0].shape[0]
    local = dot(matrix[: 3 * face], triple[...])
    for i, out in enumerate(outs):
        out[...] = local[i * face : (i + 1) * face]


def added(refs):
    value = refs[0][...]
    for ref in refs[1:]:
        value = value + ref[...]
    return value


def dual_second_kernel(matrix, flat, residual, search, image, *refs):
    parts, others, totals = refs[:4], refs[7:3:-1], refs[8:-6]
    residual_next, search_next, dense, message, old_total, triple = refs[-6:]
    face = parts[0].shape[0]
    corners = flat.shape[0]
    if totals:
        total = added(totals)
    else:
        total = parts[3][pl.ds(face, 8)] + others[3][pl.ds(face, 8)]
    old_total[...] = total
    alpha = total[:1] / total[1:2]
    gamma = cross = jnp.zeros_like(alpha)
    for i in range(4):
        here = pl.ds(i * face, face)
        older = image[here]
        first = residual[here] - alpha * older
        second = search[here] - alpha * (parts[i][:face] + others[i][:face])
        residual_next[here] = first
        search_next[here] = second
        put_triple(triple, i * face, second)
        gamma = gamma + column_sum(first, second)
        cross = cross + column_sum(second, older)
    local = dot(matrix[...], triple[...])
    dense[...] = local
    message[:corners] = dot(flat[...], triple[...])
    message[pl.ds(corners, 8)] = jnp.zeros((8, local.shape[1]), wide)
    message[pl.ds(corners, 1)] = 0.5 * gamma
    message[pl.ds(corners + 1, 1)] = 0.5 * cross
    message[pl.ds(corners + 2, 1)] = column_sum(search_next[...], local)
    message[pl.ds(corners + 3, 1)] = column_sum(search[...], local)


def coarse_back_kernel(odd, table, dense, *refs):
    every, (back_sub, back_grp, own, triple) = refs[:-4], refs[-4:]
    face = back_sub.shape[0]
    for i, message in enumerate(every):
        put_triple(triple, i * message.shape[0], message[...])
    for axis, back in enumerate((back_sub, back_grp)):
        side = odd[axis] * face
        for out, rows, place in ((back, face, face - side), (own, face, side)):
            here = pl.ds(pl.multiple_of(2 * axis * face + place, face), face)
            value = dense[here] + dot(table[here], triple[...])
            if out is own:
                own[pl.ds(axis * face, face)] = value
            else:
                out[...] = value


def final_kernel(odd, own, residual, search, image, search_next, *refs):
    (from_right, from_above), totals, (solution, final) = refs[:2], refs[2:-2], refs[-2:]
    face = from_right.shape[0]
    older = totals[0]
    newer = added(totals[1:])
    gamma, slope = older[:1], older[1:2]
    alpha = gamma / slope
    gamma_next, cross, steep, cross_other = (newer[i : i + 1] for i in range(4))
    beta = gamma_next / gamma
    alpha_next = gamma_next / (steep + beta * (cross + cross_other + beta * slope))
    for axis, back in enumerate((from_right, from_above)):
        here = pl.ds(pl.multiple_of((2 * axis + odd[axis]) * face, face), face)
        out = pl.ds(axis * face, face)
        first = search[here]
        solution[out] = alpha * first + alpha_next * (search_next[here] + beta * first)
        newest = own[out] + back[...] + beta * image[here]
        final[out] = residual[here] - alpha_next * newest


def per_device(
    jump_data,
    dual_block,
    dirichlet_block,
    coupling,
    corner_weight,
    corner_rows,
    membership,
    face_pairing,
    block_pattern,
):
    face = face_pairing.shape[-1]
    corners = corner_rows.shape[-1]
    loads = jump_data.shape[-1] // CHUNKS
    depth = 4 * face
    rows = corners + 8
    members = lax.axis_size("sub")
    ride = lax.axis_size("grp") == 4
    pattern = block_pattern[0, 0]
    pairing = face_pairing[0, 0]
    odd = jnp.stack([lax.axis_index("sub") % 2, lax.axis_index("grp") % 2]).astype(jnp.int32)
    part = ((face, loads), wide)
    more = ((face + 8, loads), wide)
    eight = ((8, loads), wide)
    whole = ((depth, loads), wide)
    triple = ((3 * depth, loads), short)
    matrix = ((depth, 3 * depth), short)
    message = ((rows, loads), wide)
    gathered = ((3 * members * rows, loads), short)
    values = ((members * rows, loads), wide)
    work = 6 * depth * depth * loads
    chunks = range(CHUNKS)

    jump = jump_data[0, 0]
    starts = []
    for i in chunks:
        columns = slice(i * loads, (i + 1) * loads)
        right, upper = jump[:face, columns], jump[face:, columns]
        from_below = move(upper, "grp", lambda i: i + 1)
        from_left = move(right, "sub", lambda i: i + 1)
        starts.append((right, upper, from_left, from_below))
    (label,) = call(
        label_kernel, [membership, corner_weight[0], corner_rows[0]], [((8, 128), wide)]
    )
    labels = gather_members(label)
    (dirichlet,) = call(
        dirichlet_kernel,
        [odd, pattern, dirichlet_block[0, 0], pairing],
        [matrix],
        flops=4 * depth * depth * depth,
        scalars=2,
    )
    steps = []
    labels[0], dirichlet, *labels[1:] = lax.optimization_barrier(
        (labels[0], dirichlet, *labels[1:])
    )
    for right, upper, from_left, from_below in starts:
        residual, field, last = call(
            start_kernel,
            [odd, dirichlet, right, upper, from_left, from_below],
            [whole, triple, part],
            flops=work // 4,
        )
        *parts, gamma_part = call(
            start_rest_kernel,
            [dirichlet, field, residual, last],
            [part] * 3 + [eight],
            flops=work,
            scalars=0,
        )
        steps.append((residual, gamma_part, parts + [last]))
    steps = [(r, g, p, swap_edges(p)) for r, g, p in steps]

    others = steps[0][3]
    odd_given, others[0] = lax.optimization_barrier((odd, others[0]))
    dual, coupling_table, coupling_flat = call(
        dual_kernel,
        [odd_given, pattern, dual_block[0, 0], pairing, coupling[0, 0].T],
        [matrix, ((depth, corners), wide), ((corners, 3 * depth), short)],
        flops=4 * depth * depth * depth,
        scalars=2,
    )
    apply_table, coarse_table = call(
        table_kernel,
        [coupling_table, *labels],
        [((depth, 3 * members * rows), short), ((members * rows, members * rows), wide)],
        [((members * rows, 128), wide)],
        scalars=0,
    )
    gamma_part, apply_table, coarse_table = lax.optimization_barrier(
        (steps[0][1], apply_table, coarse_table)
    )
    steps[0] = (steps[0][0], gamma_part, *steps[0][2:])

    firsts = []
    for residual, gamma_part, parts, others in steps:
        search, dense, sent = call(
            dual_first_kernel,
            [dual, coupling_flat, gamma_part, *parts, *others[::-1]],
            [whole, whole, message],
            [triple],
            flops=work,
            scalars=0,
        )
        firsts.append((search, dense, gather_members(sent)))
    images = []
    for _, dense, every in firsts:
        field, last = call(
            coarse_last_kernel, [apply_table, dense, *every], [gathered, part], scalars=0
        )
        *parts, total = call(
            coarse_rest_kernel,
            [apply_table, dense, field, coarse_table, *every],
            [part, part, more, eight],
            [values],
            scalars=0,
        )
        images.append((total, parts + [last], swap_edges(parts + [last])))
    seconds = []
    for total, parts, others in images:
        image, field, last = call(
            second_last_kernel,
            [dirichlet, total, *parts, *others[::-1]],
            [whole, triple, more],
            flops=work // 4,
            scalars=0,
        )
        parts = call(second_rest_kernel, [dirichlet, field], [part] * 3, flops=work, scalars=0)
        parts = list(parts) + [last]
        totals = [] if ride else group_terms(total)
        seconds.append((image, totals, parts, swap_edges(parts)))
    thirds = []
    for (residual, *_), (search, *_), (image, totals, parts, others) in zip(steps, firsts, seconds):
        *kept, sent, old_total = call(
            dual_second_kernel,
            [dual, coupling_flat, residual, search, image, *parts, *others[::-1], *totals],
            [whole, whole, whole, message, eight],
            [triple],
            flops=work,
            scalars=0,
        )
        thirds.append((*kept, old_total, gather_members(sent)))
    results = []
    for (search, _, older), (image, *_), (residual, search_next, dense, old_total, every) in zip(
        firsts, seconds, thirds
    ):
        (total,) = call(
            functools.partial(energy_kernel, members),
            [coarse_table, *every, *older],
            [eight],
            [values],
            scalars=0,
        )
        totals = group_terms(total)
        back_sub, back_grp, own = call(
            coarse_back_kernel,
            [odd, apply_table, dense, *every],
            [part, part, ((2 * face, loads), wide)],
            [gathered],
        )
        from_above = move(back_grp, "grp", lambda i: i - 1)
        from_right = move(back_sub, "sub", lambda i: i - 1)
        results.append(
            call(
                final_kernel,
                [
                    odd,
                    own,
                    residual,
                    search,
                    image,
                    search_next,
                    from_right,
                    from_above,
                    old_total,
                    *totals,
                ],
                [((2 * face, loads), wide)] * 2,
            )
        )
    if CHUNKS > 1:
        results = [[jnp.concatenate(pieces, 1) for pieces in zip(*results)]]
    (solution, final) = results[0]
    return (solution[None, None], final[None, None])


def solution(mesh):
    placed = (
        P("grp", "sub", None, None),
        P("grp", "sub", None, None),
        P("grp", "sub", None, None),
        P("grp", "sub", None, None),
        P("grp", "sub", None),
        P("grp", "sub", None),
        P("grp", "sub"),
        P("grp", "sub", None, None),
        P("grp", "sub", None, None),
    )
    return jax.shard_map(
        per_device,
        mesh=mesh,
        in_specs=placed,
        out_specs=(P("grp", "sub", None, None), P("grp", "sub", None, None)),
        check_vma=False,
    )
```

```python
import functools

import jax
import jax.numpy as jnp
from jax import lax
from jax.experimental import pallas as pl
from jax.experimental.pallas import tpu as pltpu
from jax.sharding import PartitionSpec as P

ITERS = 2
LIMIT = 8 * 1024 * 1024

VMEM = pl.BlockSpec(memory_space=pltpu.VMEM)
SMEM = pl.BlockSpec(memory_space=pltpu.SMEM)
wide = jnp.float32
short = jnp.bfloat16
highest = lax.Precision.HIGHEST


def call(body, inputs, outputs, scratch=(), flops=0, scalars=1):
    moved = sum(x.size * x.dtype.itemsize for x in inputs)
    return pl.pallas_call(
        body,
        out_shape=[jax.ShapeDtypeStruct(shape, kind) for shape, kind in outputs],
        in_specs=[SMEM] * scalars + [VMEM] * (len(inputs) - scalars),
        out_specs=[VMEM] * len(outputs),
        scratch_shapes=[pltpu.VMEM(shape, kind) for shape, kind in scratch],
        compiler_params=pltpu.CompilerParams(vmem_limit_bytes=LIMIT),
        cost_estimate=pl.CostEstimate(flops=flops, bytes_accessed=moved, transcendentals=0),
    )(*inputs)


def move(array, axis, target):
    peers = lax.axis_size(axis)
    return lax.ppermute(array, axis, [(i, target(i) % peers) for i in range(peers)])


def near(i):
    return i ^ 1


def far(i):
    return i - 1 if i % 2 == 0 else i + 1


def swap_edges(parts):
    return [
        move(parts[0], "sub", near),
        move(parts[1], "sub", far),
        move(parts[2], "grp", near),
        move(parts[3], "grp", far),
    ]


def gather_members(array):
    return lax.all_gather(array, "sub", axis=0, tiled=True)


def group_terms(array):
    peers = lax.axis_size("grp")
    if peers <= 4:
        return [array] + [move(array, "grp", lambda i, k=k: i + k) for k in range(1, peers)]
    step = 1
    while step < peers:
        array = array + move(array, "grp", lambda i, k=step: i ^ k)
        step *= 2
    return [array]


def dot(first, second, precision=None):
    return jnp.dot(first, second, precision=precision, preferred_element_type=wide)


def dot_across(first, second):
    return lax.dot_general(first, second, (((1,), (1,)), ((), ())), preferred_element_type=wide)


def halves(value):
    high = value.astype(short)
    return high, (value - high.astype(wide)).astype(short)


def put_triple(ref, rows, value, base=0, depth=None):
    depth = depth or ref.shape[0] // 3
    high, low = halves(value)
    for i, part in enumerate((high, low, high)):
        ref[pl.ds(base + i * depth + rows, value.shape[0])] = part


def parities():
    return lax.axis_index("sub") % 2, lax.axis_index("grp") % 2


def far_sub():
    sub, peers = lax.axis_index("sub"), lax.axis_size("sub")
    return lax.rem(jnp.where(sub % 2 == 1, sub + 1, sub + peers - 1), peers)


def column_sum(first, second):
    return jnp.sum(first * second, axis=0, keepdims=True)


def turning(odd, pairing):
    face = pairing.shape[-1]
    place = lax.broadcasted_iota(jnp.int32, (face, face), 0)
    table = jnp.where(place == pairing, -1.0, 0.0)
    identity = jnp.where(place == lax.broadcasted_iota(jnp.int32, (face, face), 1), 1.0, 0.0)
    chosen = jnp.where(odd == 1, 1.0, 0.0)
    top = jnp.concatenate([identity * (1.0 - chosen), table * chosen], 1)
    bottom = jnp.concatenate([identity * chosen, table * (1.0 - chosen)], 1)
    return jnp.concatenate([top, bottom], 0).astype(short)


def turn_block(pattern, block, pairing, out):
    face = pairing.shape[-1]
    pair = 2 * face
    odd = parities()
    turns = [turning(odd[a], pairing[a : a + 1]) for a in range(2)]
    for a in range(2):
        for b in range(2):
            rows = []
            for i in range(2):
                rows.append(
                    jnp.concatenate(
                        [
                            block[
                                pl.ds((2 * a + i) * face, face), pl.ds((2 * b + j) * face, face)
                            ]
                            * pattern[2 * a + i, 2 * b + j].astype(wide)
                            for j in range(2)
                        ],
                        1,
                    )
                )
            for k, part in enumerate(halves(jnp.concatenate(rows, 0))):
                part = dot_across(dot(turns[a], part).astype(short), turns[b]).astype(short)
                here = pl.ds(a * pair, pair)
                for i in (0, 1) if k == 0 else (2,):
                    out[here, pl.ds((3 * b + i) * pair, pair)] = part
    return turns


def dual_kernel(pattern, block, pairing, out):
    turn_block(pattern, block, pairing, out)


def put_table(out, rows, value):
    high, low = halves(value)
    width = value.shape[1]
    for i, part in enumerate((high, high, low)):
        out[rows, pl.ds(32 * i, width)] = part


def put_values(out, value):
    high, low = halves(value)
    for i, part in enumerate((high, low, high)):
        out[pl.ds(32 * i, 32)] = part
    out[pl.ds(96, 32)] = jnp.zeros((32, value.shape[1]), short)


def dirichlet_kernel(pattern, block, pairing, coupling, out, flat, table, *slips):
    every_turn = turn_block(pattern, block, pairing, out)
    face = pairing.shape[-1]
    pair = 2 * face
    table[...] = jnp.zeros(table.shape, short)
    for a, turns in enumerate(every_turn):
        here = pl.ds(a * pair, pair)
        high, low = (dot_across(v, turns) for v in halves(coupling[:, here]))
        for i, half in enumerate((high, high, low)):
            flat[:, pl.ds((3 * a + i) * pair, pair)] = half.astype(short)
        total = high + low
        put_table(table, here, total.T)
        for i in range(2):
            slip = slips[2 * a + i]
            slip[...] = jnp.zeros(slip.shape, wide)
            for k in range(coupling.shape[0] // 8):
                slip[:, pl.ds(k * face, face)] = total[
                    8 * k : 8 * k + 8, i * face : (i + 1) * face
                ]


def neighbour_kernel(corners, *refs):
    for message, out in zip(refs[:2], refs[2:]):
        face = out.shape[0]
        slip = message[pl.ds(face, 8)]
        parts = [slip[:, k * face : (k + 1) * face] for k in range(corners // 8)]
        out[...] = jnp.zeros(out.shape, short)
        put_table(out, pl.ds(0, face), jnp.concatenate(parts, 0).T)


def label_kernel(member, weight, rows, out):
    corners = rows.shape[-1]
    out[...] = jnp.full(out.shape, -1.0, wide)
    out[:1, :corners] = weight[...]
    out[1:2, :corners] = rows[...].astype(wide)
    out[2:3, :corners] = jnp.full((1, corners), member[0, 0].astype(wide))


def table_kernel(labels, table, columns):
    rows = 32
    columns[...] = jnp.zeros(columns.shape, wide)
    for i in range(labels.shape[0] // 8):
        columns[pl.ds(i * rows, rows), :8] = labels[pl.ds(8 * i, 8)].T[:rows]
    across = columns[...].T
    weight, row, member = (across[i : i + 1] for i in range(3))
    same = (columns[:, 1:2] == row) & (columns[:, 2:3] == member) & (columns[:, 1:2] >= 0)
    linked = jnp.where(same, 1.0, 0.0)
    total = jnp.sum(linked * weight, axis=1, keepdims=True)
    high, low = halves(linked / jnp.where(total > 0, total, 1.0))
    width = table.shape[0]
    table[:, :width] = high
    table[:, width : 2 * width] = high
    table[:, 2 * width :] = low


def start_kernel(matrix, right, upper, from_left, from_below, field, triple, last):
    face = from_left.shape[0]
    odd = parities()
    for axis, (own, other) in enumerate(((right, from_left), (upper, from_below))):
        here = pl.ds(2 * axis * face, face)
        there = pl.ds((2 * axis + 1) * face, face)
        first = jnp.where(odd[axis] == 1, other[...], own[...])
        second = jnp.where(odd[axis] == 1, own[...], other[...])
        field[here] = first
        field[there] = second
        put_triple(triple, 0, first, 6 * axis * face, 2 * face)
        put_triple(triple, face, second, 6 * axis * face, 2 * face)
    last[...] = dot(matrix[pl.ds(3 * face, face)], triple[...])


def start_rest_kernel(matrix, triple, field, last, *refs):
    slips, (first, second, third, fourth, sums) = refs[:4], refs[4:]
    face = last.shape[0]
    total = column_sum(field[pl.ds(3 * face, face)], last[...])
    local = dot(matrix[: 3 * face], triple[...])
    for i, out in enumerate((first, second, third)):
        out[:face] = local[i * face : (i + 1) * face]
    fourth[:face] = last[...]
    for out, slip in zip((first, second, third, fourth), slips):
        out[pl.ds(face, 8)] = slip[...]
    sums[...] = jnp.broadcast_to(total + column_sum(field[: 3 * face], local), sums.shape)


def both_dots(matrix, *triples):
    width = triples[0].shape[0]
    return dot(matrix[:, :width], triples[0][...]) + dot(matrix[:, width:], triples[1][...])


def edges_kernel(third, fourth, far_one, near_one, field, triple):
    face = far_one.shape[0] - 8
    for i, (part, other) in enumerate(((third, near_one), (fourth, far_one))):
        value = part[:face] + other[:face]
        field[pl.ds(i * face, face)] = value
        put_triple(triple, i * face, value)


def dual_first_kernel(matrix, flat, gamma, field_grp, triple_grp, *refs):
    parts, others, (field, *outs, message, triple) = refs[:2], refs[2:4], refs[4:]
    face = outs[0].shape[0]
    corners = flat.shape[0]
    for i in range(2):
        value = parts[i][:face] + others[i][:face]
        field[pl.ds(i * face, face)] = value
        put_triple(triple, i * face, value)
    field[pl.ds(2 * face, 2 * face)] = field_grp[...]
    local = both_dots(matrix, triple, triple_grp)
    for i, out in enumerate(outs):
        out[...] = local[i * face : (i + 1) * face]
    message[:corners] = both_dots(flat, triple, triple_grp)
    message[pl.ds(corners, 8)] = jnp.zeros((8, field.shape[1]), wide)
    message[pl.ds(corners, 1)] = gamma[:1]
    message[pl.ds(corners + 1, 1)] = column_sum(field[...], local)


def coarse_kernel(corners, second, table, coupling, near_table, far_table, *refs):
    count = 2 if second else 1
    every, (passed, extra, triple, coarse, values) = refs[:count], refs[count:]
    rows = passed.shape[0]
    face = near_table.shape[0]
    put_triple(triple, 0, every[0][...])
    coarse[...] = dot(table[...], triple[...])
    sums = jnp.zeros((8, passed.shape[1]), wide)
    extras = [jnp.zeros((1, passed.shape[1]), wide) for _ in range(count)]
    for i in range(every[0].shape[0] // rows):
        here = pl.ds(i * rows, corners)
        sums = sums + every[0][pl.ds(i * rows + corners, 8)]
        for j in range(count):
            extras[j] = extras[j] + column_sum(coarse[here], every[j][here])
    sub = lax.axis_index("sub")
    own, partner, other = (
        pl.ds(pl.multiple_of(place * rows, rows), rows) for place in (sub, sub ^ 1, far_sub())
    )
    passed[...] = coarse[own]
    passed[pl.ds(corners, 8)] = sums
    for j, one in enumerate(extras):
        place = count + j
        passed[pl.ds(corners + place, 1)] = sums[place : place + 1] + one
    put_values(values, coarse[own])
    extra[...] = dot(coupling[...], values[...])
    put_values(values, coarse[partner])
    extra[:face] += dot(near_table[...], values[...])
    put_values(values, coarse[other])
    extra[pl.ds(face, face)] += dot(far_table[...], values[...])


def second_edges_kernel(corners, *refs):
    (extra, near_table, far_table, passed, near_passed, far_passed, *refs) = refs
    (third, fourth, far_one, near_one, field, triple, passing, sums, values) = refs
    face = third.shape[0]
    sides = ((third, near_one, near_table, near_passed), (fourth, far_one, far_table, far_passed))
    for i, (part, other, table, more) in enumerate(sides):
        put_values(values, more[...])
        value = part[...] + other[...] + extra[pl.ds((2 + i) * face, face)]
        value = value + dot(table[...], values[...])
        field[pl.ds(i * face, face)] = value
        put_triple(triple, i * face, value)
    eight = pl.ds(corners, 8)
    passing[...] = far_passed[eight]
    sums[...] = passed[eight] + near_passed[eight] + far_passed[eight]


def second_kernel(matrix, extra, passing, field_grp, triple_grp, *refs):
    parts, others, (field, *outs, triple) = refs[:2], refs[2:4], refs[4:]
    face = parts[0].shape[0]
    for i in range(2):
        here = pl.ds(i * face, face)
        value = parts[i][...] + others[i][...] + extra[here]
        field[here] = value
        put_triple(triple, i * face, value)
    field[pl.ds(2 * face, 2 * face)] = field_grp[...]
    local = both_dots(matrix, triple, triple_grp)
    for i, out in enumerate(outs):
        out[:face] = local[i * face : (i + 1) * face]
    outs[2][pl.ds(face, 8)] = passing[...]


def added(refs):
    value = refs[0][...]
    for ref in refs[1:]:
        value = value + ref[...]
    return value


def step_rows(total, residual, search, image, later, rows, residual_next, search_next):
    alpha = total[:1] / total[1:2]
    older = image[rows]
    first = residual[rows] - alpha * older
    second = search[rows] - alpha * later
    residual_next[...] = first
    search_next[...] = second
    return second, column_sum(first, second), column_sum(second, older)


def step_edges_kernel(residual, search, image, third, fourth, far_one, near_one, *refs):
    totals, (residual_next, search_next, triple, total, sums) = refs[:-5], refs[-5:]
    face = third.shape[0] - 8
    value = added(totals)
    if near_one.shape[0] > face:
        value = value + near_one[pl.ds(face, 8)]
    total[...] = value
    sums[...] = jnp.zeros(sums.shape, wide)
    for i, later in enumerate((third[:face] + near_one[:face], fourth[...] + far_one[...])):
        here = pl.ds(i * face, face)
        second, gamma, cross = step_rows(
            value,
            residual,
            search,
            image,
            later,
            pl.ds((2 + i) * face, face),
            residual_next.at[here],
            search_next.at[here],
        )
        put_triple(triple, i * face, second)
        sums[:1] += gamma
        sums[1:2] += cross


def step_kernel(matrix, flat, residual, search, image, total, *refs):
    (grp_residual, grp_search, triple_grp, grp_sums, *parts) = refs[:8]
    residual_next, search_next, back_sub, back_grp, dense, message, triple = refs[8:]
    face = back_sub.shape[0]
    corners = flat.shape[0]
    odd = parities()
    sums = grp_sums[:2]
    for i in range(2):
        here = pl.ds(i * face, face)
        second, gamma, cross = step_rows(
            total[...],
            residual,
            search,
            image,
            parts[i][...] + parts[2 + i][...],
            here,
            residual_next.at[here],
            search_next.at[here],
        )
        put_triple(triple, i * face, second)
        sums = sums + jnp.concatenate([gamma, cross], 0)
    half = pl.ds(2 * face, 2 * face)
    residual_next[half] = grp_residual[...]
    search_next[half] = grp_search[...]
    local = both_dots(matrix, triple, triple_grp)
    dense[...] = local
    for axis, back in enumerate((back_sub, back_grp)):
        here = pl.ds(pl.multiple_of((2 * axis + 1 - odd[axis]) * face, face), face)
        back[...] = dense[here]
    message[:corners] = both_dots(flat, triple, triple_grp)
    message[pl.ds(corners, 8)] = jnp.zeros((8, local.shape[1]), wide)
    message[pl.ds(corners, 2)] = 0.5 * sums
    message[pl.ds(corners + 2, 1)] = column_sum(search_next[...], local)
    message[pl.ds(corners + 3, 1)] = column_sum(search[...], local)


def owned_kernel(*refs):
    half = len(refs) // 2
    odd = parities()
    for whole, own in zip(refs[:half], refs[half:]):
        face = own.shape[0] // 2
        for axis in range(2):
            here = pl.ds(pl.multiple_of((2 * axis + odd[axis]) * face, face), face)
            own[pl.ds(axis * face, face)] = whole[here]


def final_kernel(corners, *refs):
    (residual, search, image, search_next, dense, extra, near_table, far_table, *refs) = refs
    from_right, from_above, old_total, near_passed, far_passed, *refs = refs
    totals, (solution, final, values) = refs[:-3], refs[-3:]
    face = from_right.shape[0]
    odd = parities()
    newer = added(totals)
    if len(totals) > 1:
        newer = newer[-8:] + near_passed[pl.ds(corners, 8)] + far_passed[pl.ds(corners, 8)]
    gamma, slope = old_total[:1], old_total[1:2]
    alpha = gamma / slope
    gamma_next, cross, steep, cross_other = (newer[i : i + 1] for i in range(4))
    beta = gamma_next / gamma
    alpha_next = gamma_next / (steep + beta * (cross + cross_other + beta * slope))
    upper = odd[1] == 1
    table = jnp.where(upper, far_table[...].astype(wide), near_table[...].astype(wide))
    put_values(values, jnp.where(upper, far_passed[...], near_passed[...]))
    last = dot(table.astype(short), values[...])
    for axis, back in enumerate((from_right, from_above)):
        here = pl.ds(pl.multiple_of((2 * axis + odd[axis]) * face, face), face)
        out = pl.ds(axis * face, face)
        first = search[out]
        solution[out] = alpha * first + alpha_next * (search_next[out] + beta * first)
        newest = dense[out] + extra[here] + back[...] + beta * image[out]
        if axis == 1:
            newest = newest + last
        final[out] = residual[out] - alpha_next * newest


def per_device(
    jump_data,
    dual_block,
    dirichlet_block,
    coupling,
    corner_weight,
    corner_rows,
    membership,
    face_pairing,
    block_pattern,
):
    face = face_pairing.shape[-1]
    corners = corner_rows.shape[-1]
    loads = jump_data.shape[-1]
    depth = 4 * face
    rows = corners + 8
    members = lax.axis_size("sub")
    ride = lax.axis_size("grp") == 4
    pattern = block_pattern[0, 0]
    pairing = face_pairing[0, 0]
    part = ((face, loads), wide)
    more = ((face + 8, loads), wide)
    eight = ((8, loads), wide)
    whole = ((depth, loads), wide)
    triple = ((3 * depth, loads), short)
    half = ((2 * face, loads), wide)
    half_triple = ((6 * face, loads), short)
    matrix = ((depth, 3 * depth), short)
    message = ((rows, loads), wide)
    gathered = ((members * rows, loads), wide)
    gathered_triple = ((3 * members * rows, loads), short)
    values = ((128, loads), short)
    table = ((face, 128), short)
    work = 6 * depth * depth * loads
    turn_work = 4 * depth * depth * depth

    jump = jump_data[0, 0]
    right, upper = jump[:face], jump[face:]
    from_below = move(upper, "grp", lambda i: i + 1)
    from_left = move(right, "sub", lambda i: i + 1)
    (label,) = call(
        label_kernel, [membership, corner_weight[0], corner_rows[0]], [((8, 128), wide)]
    )
    dirichlet, coupling_flat, coupling_table, *slips = call(
        dirichlet_kernel,
        [pattern, dirichlet_block[0, 0], pairing, coupling[0, 0].T],
        [matrix, ((corners, 3 * depth), short), ((depth, 128), short)] + [eight] * 4,
        flops=turn_work,
    )
    (dual,) = call(
        dual_kernel,
        [pattern, dual_block[0, 0], pairing],
        [matrix],
        flops=turn_work,
    )
    dirichlet, dual = lax.optimization_barrier((dirichlet, dual))
    residual, field, last = call(
        start_kernel,
        [dirichlet, right, upper, from_left, from_below],
        [whole, triple, part],
        flops=work // 4,
        scalars=0,
    )
    *parts, gamma_part = call(
        start_rest_kernel,
        [dirichlet, field, residual, last, *slips],
        [more] * 4 + [eight],
        flops=work,
        scalars=0,
    )

    others = swap_edges(parts)
    others[0], label_given = lax.optimization_barrier((others[0], label))
    labels = gather_members(label_given)
    (coarse_table,) = call(
        table_kernel,
        [labels],
        [((members * rows, 3 * members * rows), short)],
        [((members * rows, 128), wide)],
        scalars=0,
    )
    gamma_part, coarse_table = lax.optimization_barrier((gamma_part, coarse_table))

    edges = call(
        edges_kernel, [*parts[2:], others[3], others[2]], [half, half_triple], scalars=0
    )
    search, *image_parts, sent = call(
        dual_first_kernel,
        [dual, coupling_flat, gamma_part, *edges, *parts[:2], *others[:2]],
        [whole] + [part] * 4 + [message],
        [half_triple],
        flops=work,
        scalars=0,
    )
    first = move(image_parts[0], "sub", near)
    third, fourth = move(image_parts[2], "grp", near), move(image_parts[3], "grp", far)
    first, sent = lax.optimization_barrier((first, sent))
    every = gather_members(sent)
    image_parts[1], every = lax.optimization_barrier((image_parts[1], every))
    image_others = [first, move(image_parts[1], "sub", far), third, fourth]
    tables = []
    for axis in range(2):
        tables += call(
            functools.partial(neighbour_kernel, corners),
            others[2 * axis : 2 * axis + 2],
            [table] * 2,
            scalars=0,
        )
    passed, extra = call(
        functools.partial(coarse_kernel, corners, False),
        [coarse_table, coupling_table, *tables[:2], every],
        [message, whole],
        [gathered_triple, gathered, values],
        scalars=0,
    )
    near_passed, far_passed = move(passed, "grp", near), move(passed, "grp", far)
    *edges, passing, sums = call(
        functools.partial(second_edges_kernel, corners),
        [
            extra,
            *tables[2:],
            passed,
            near_passed,
            far_passed,
            *image_parts[2:],
            image_others[3],
            image_others[2],
        ],
        [half, half_triple, eight, eight],
        [values],
        scalars=0,
    )
    image, *later_parts = call(
        second_kernel,
        [dirichlet, extra, passing, *edges, *image_parts[:2], *image_others[:2]],
        [whole, part, part, more, part],
        [half_triple],
        flops=work,
        scalars=0,
    )
    later_others = swap_edges(later_parts)
    totals = [sums] if ride else group_terms(passed[corners:])
    if not ride:
        later_others[2] = later_others[2][:face]
    *edges, old_total, grp_sums = call(
        step_edges_kernel,
        [residual, search, image, *later_parts[2:], later_others[3], later_others[2], *totals],
        [half, half, half_triple, eight, eight],
        scalars=0,
    )
    residual_next, search_next, back_sub, back_grp, dense, sent = call(
        step_kernel,
        [
            dual,
            coupling_flat,
            residual,
            search,
            image,
            old_total,
            *edges,
            grp_sums,
            *later_parts[:2],
            *later_others[:2],
        ],
        [whole, whole, part, part, whole, message],
        [half_triple],
        flops=work,
        scalars=0,
    )
    from_above = move(back_grp, "grp", lambda i: i - 1)
    every_next = gather_members(sent)
    back_sub, every_next = lax.optimization_barrier((back_sub, every_next))
    from_right = move(back_sub, "sub", lambda i: i - 1)
    passed, extra = call(
        functools.partial(coarse_kernel, corners, True),
        [coarse_table, coupling_table, *tables[:2], every_next, every],
        [message, whole],
        [gathered_triple, gathered, values],
        scalars=0,
    )
    near_passed, far_passed = move(passed, "grp", near), move(passed, "grp", far)
    if ride:
        totals = [passed[corners:], move(passed[corners:], "grp", lambda i: i ^ 2)]
    else:
        totals = group_terms(passed[corners:])
    owned = []
    for arrays in ((residual_next, search), (image, search_next, dense)):
        owned += call(
            owned_kernel,
            arrays,
            [((2 * face, loads), wide)] * len(arrays),
            flops=0,
            scalars=0,
        )
    solution, final = call(
        functools.partial(final_kernel, corners),
        [
            *owned,
            extra,
            *tables[2:],
            from_right,
            from_above,
            old_total,
            near_passed,
            far_passed,
            *totals,
        ],
        [((2 * face, loads), wide)] * 2,
        [values],
        scalars=0,
    )
    return (solution[None, None], final[None, None])


def solution(mesh):
    placed = (
        P("grp", "sub", None, None),
        P("grp", "sub", None, None),
        P("grp", "sub", None, None),
        P("grp", "sub", None, None),
        P("grp", "sub", None),
        P("grp", "sub", None),
        P("grp", "sub"),
        P("grp", "sub", None, None),
        P("grp", "sub", None, None),
    )
    return jax.shard_map(
        per_device,
        mesh=mesh,
        in_specs=placed,
        out_specs=(P("grp", "sub", None, None), P("grp", "sub", None, None)),
        check_vma=False,
    )
```

```python
import functools

import jax
import jax.numpy as jnp
from jax import lax
from jax.experimental import pallas as pl
from jax.experimental.pallas import tpu as pltpu
from jax.sharding import PartitionSpec as P

ITERS = 2
LIMIT = 8 * 1024 * 1024

VMEM = pl.BlockSpec(memory_space=pltpu.VMEM)
SMEM = pl.BlockSpec(memory_space=pltpu.SMEM)
wide = jnp.float32
short = jnp.bfloat16
highest = lax.Precision.HIGHEST


def call(body, inputs, outputs, scratch=(), flops=0, scalars=1):
    moved = sum(x.size * x.dtype.itemsize for x in inputs)
    return pl.pallas_call(
        body,
        out_shape=[jax.ShapeDtypeStruct(shape, kind) for shape, kind in outputs],
        in_specs=[SMEM] * scalars + [VMEM] * (len(inputs) - scalars),
        out_specs=[VMEM] * len(outputs),
        scratch_shapes=[pltpu.VMEM(shape, kind) for shape, kind in scratch],
        compiler_params=pltpu.CompilerParams(vmem_limit_bytes=LIMIT),
        cost_estimate=pl.CostEstimate(flops=flops, bytes_accessed=moved, transcendentals=0),
    )(*inputs)


def move(array, axis, target):
    peers = lax.axis_size(axis)
    return lax.ppermute(array, axis, [(i, target(i) % peers) for i in range(peers)])


def near(i):
    return i ^ 1


def far(i):
    return i - 1 if i % 2 == 0 else i + 1


def swap_edges(parts):
    return [
        move(parts[0], "sub", near),
        move(parts[1], "sub", far),
        move(parts[2], "grp", near),
        move(parts[3], "grp", far),
    ]


def gather_members(array):
    peers = lax.axis_size("sub")
    same = [array] + [move(array, "sub", lambda i, k=k: i ^ k) for k in range(2, peers, 2)]
    return same + [move(one, "sub", near) for one in same]


def order_of_members(peers):
    return [*range(0, peers, 2), *range(1, peers, 2)]


def member_rows(distance, rows):
    return pl.ds(pl.multiple_of((lax.axis_index("sub") ^ distance) * rows, rows), rows)


def group_terms(array):
    peers = lax.axis_size("grp")
    if peers <= 4:
        return [array] + [move(array, "grp", lambda i, k=k: i + k) for k in range(1, peers)]
    step = 1
    while step < peers:
        array = array + move(array, "grp", lambda i, k=step: i ^ k)
        step *= 2
    return [array]


def dot(first, second, precision=None):
    return jnp.dot(first, second, precision=precision, preferred_element_type=wide)


def dot_across(first, second):
    return lax.dot_general(first, second, (((1,), (1,)), ((), ())), preferred_element_type=wide)


def halves(value):
    high = value.astype(short)
    return high, (value - high.astype(wide)).astype(short)


def put_triple(ref, rows, value, base=0, depth=None):
    depth = depth or ref.shape[0] // 3
    high, low = halves(value)
    for i, part in enumerate((high, low, high)):
        ref[pl.ds(base + i * depth + rows, value.shape[0])] = part


def parities():
    return lax.axis_index("sub") % 2, lax.axis_index("grp") % 2


def far_sub():
    sub, peers = lax.axis_index("sub"), lax.axis_size("sub")
    return lax.rem(jnp.where(sub % 2 == 1, sub + 1, sub + peers - 1), peers)


def column_sum(first, second):
    return jnp.sum(first * second, axis=0, keepdims=True)


def turning(odd, pairing):
    face = pairing.shape[-1]
    place = lax.broadcasted_iota(jnp.int32, (face, face), 0)
    table = jnp.where(place == pairing, -1.0, 0.0)
    identity = jnp.where(place == lax.broadcasted_iota(jnp.int32, (face, face), 1), 1.0, 0.0)
    chosen = jnp.where(odd == 1, 1.0, 0.0)
    top = jnp.concatenate([identity * (1.0 - chosen), table * chosen], 1)
    bottom = jnp.concatenate([identity * chosen, table * (1.0 - chosen)], 1)
    return jnp.concatenate([top, bottom], 0).astype(short)


def turn_block(pattern, block, pairing, out):
    face = pairing.shape[-1]
    pair = 2 * face
    odd = parities()
    turns = [turning(odd[a], pairing[a : a + 1]) for a in range(2)]
    for a in range(2):
        for b in range(2):
            rows = []
            for i in range(2):
                rows.append(
                    jnp.concatenate(
                        [
                            block[
                                pl.ds((2 * a + i) * face, face), pl.ds((2 * b + j) * face, face)
                            ]
                            * pattern[2 * a + i, 2 * b + j].astype(wide)
                            for j in range(2)
                        ],
                        1,
                    )
                )
            for k, part in enumerate(halves(jnp.concatenate(rows, 0))):
                part = dot_across(dot(turns[a], part).astype(short), turns[b]).astype(short)
                here = pl.ds(a * pair, pair)
                for i in (0, 1) if k == 0 else (2,):
                    out[here, pl.ds((3 * b + i) * pair, pair)] = part
    return turns


def dual_kernel(pattern, block, pairing, out):
    turn_block(pattern, block, pairing, out)


def put_table(out, rows, value):
    high, low = halves(value)
    width = value.shape[1]
    for i, part in enumerate((high, high, low)):
        out[rows, pl.ds(32 * i, width)] = part


def put_values(out, value):
    high, low = halves(value)
    for i, part in enumerate((high, low, high)):
        out[pl.ds(32 * i, 32)] = part
    out[pl.ds(96, 32)] = jnp.zeros((32, value.shape[1]), short)


def dirichlet_kernel(pattern, block, pairing, coupling, out, flat, table, *slips):
    every_turn = turn_block(pattern, block, pairing, out)
    face = pairing.shape[-1]
    pair = 2 * face
    table[...] = jnp.zeros(table.shape, short)
    for a, turns in enumerate(every_turn):
        here = pl.ds(a * pair, pair)
        high, low = (dot_across(v, turns) for v in halves(coupling[:, here]))
        for i, half in enumerate((high, high, low)):
            flat[:, pl.ds((3 * a + i) * pair, pair)] = half.astype(short)
        total = high + low
        put_table(table, here, total.T)
        for i in range(2):
            slip = slips[2 * a + i]
            slip[...] = jnp.zeros(slip.shape, wide)
            for k in range(coupling.shape[0] // 8):
                slip[:, pl.ds(k * face, face)] = total[
                    8 * k : 8 * k + 8, i * face : (i + 1) * face
                ]


def neighbour_kernel(corners, *refs):
    for message, out in zip(refs[:2], refs[2:]):
        face = out.shape[0]
        slip = message[pl.ds(face, 8)]
        parts = [slip[:, k * face : (k + 1) * face] for k in range(corners // 8)]
        out[...] = jnp.zeros(out.shape, short)
        put_table(out, pl.ds(0, face), jnp.concatenate(parts, 0).T)


def label_kernel(member, weight, rows, out):
    corners = rows.shape[-1]
    out[...] = jnp.full(out.shape, -1.0, wide)
    out[:1, :corners] = weight[...]
    out[1:2, :corners] = rows[...].astype(wide)
    out[2:3, :corners] = jnp.full((1, corners), member[0, 0].astype(wide))


def table_kernel(labels, table, columns):
    rows = 32
    columns[...] = jnp.zeros(columns.shape, wide)
    for i, distance in enumerate(order_of_members(labels.shape[0] // 8)):
        columns[pl.ds(i * rows, rows), :8] = labels[member_rows(distance, 8)].T[:rows]
    across = columns[...].T
    weight, row, member = (across[i : i + 1] for i in range(3))
    same = (columns[:, 1:2] == row) & (columns[:, 2:3] == member) & (columns[:, 1:2] >= 0)
    linked = jnp.where(same, 1.0, 0.0)
    total = jnp.sum(linked * weight, axis=1, keepdims=True)
    high, low = halves(linked / jnp.where(total > 0, total, 1.0))
    width = table.shape[0]
    table[:, :width] = high
    table[:, width : 2 * width] = high
    table[:, 2 * width :] = low


def start_kernel(matrix, right, upper, from_left, from_below, *refs):
    slips, (field, first, second, third, fourth, sums, triple) = refs[:4], refs[4:]
    face = from_left.shape[0]
    odd = parities()
    for axis, (own, other) in enumerate(((right, from_left), (upper, from_below))):
        here = pl.ds(2 * axis * face, face)
        there = pl.ds((2 * axis + 1) * face, face)
        one = jnp.where(odd[axis] == 1, other[...], own[...])
        two = jnp.where(odd[axis] == 1, own[...], other[...])
        field[here] = one
        field[there] = two
        put_triple(triple, 0, one, 6 * axis * face, 2 * face)
        put_triple(triple, face, two, 6 * axis * face, 2 * face)
    local = dot(matrix[...], triple[...])
    for i, (out, slip) in enumerate(zip((first, second, third, fourth), slips)):
        out[:face] = local[i * face : (i + 1) * face]
        out[pl.ds(face, 8)] = slip[...]
    sums[...] = jnp.broadcast_to(column_sum(field[...], local), sums.shape)


def both_dots(matrix, *triples):
    width = triples[0].shape[0]
    return dot(matrix[:, :width], triples[0][...]) + dot(matrix[:, width:], triples[1][...])


def edges_kernel(third, fourth, far_one, near_one, field, triple):
    face = far_one.shape[0] - 8
    for i, (part, other) in enumerate(((third, near_one), (fourth, far_one))):
        value = part[:face] + other[:face]
        field[pl.ds(i * face, face)] = value
        put_triple(triple, i * face, value)


def dual_first_kernel(matrix, flat, gamma, field_grp, triple_grp, *refs):
    parts, others, (field, *outs, message, triple) = refs[:2], refs[2:4], refs[4:]
    face = outs[0].shape[0]
    corners = flat.shape[0]
    for i in range(2):
        value = parts[i][:face] + others[i][:face]
        field[pl.ds(i * face, face)] = value
        put_triple(triple, i * face, value)
    field[pl.ds(2 * face, 2 * face)] = field_grp[...]
    local = both_dots(matrix, triple, triple_grp)
    for i, out in enumerate(outs):
        out[...] = local[i * face : (i + 1) * face]
    message[:corners] = both_dots(flat, triple, triple_grp)
    message[pl.ds(corners, 8)] = jnp.zeros((8, field.shape[1]), wide)
    message[pl.ds(corners, 1)] = gamma[:1]
    message[pl.ds(corners + 1, 1)] = column_sum(field[...], local)


def coarse_kernel(corners, table, *refs):
    *every, first_every, passed, coarse, triple = refs
    rows = passed.shape[0]
    members = first_every.shape[0] // rows
    older = [first_every.at[member_rows(d, rows)] for d in order_of_members(members)]
    groups = [every, older] if every else [older]
    count = len(groups)
    for i in range(members):
        put_triple(triple, i * rows, groups[0][i][...])
    coarse[...] = dot(table[...], triple[...])
    sums = jnp.zeros((8, passed.shape[1]), wide)
    extras = [jnp.zeros((1, passed.shape[1]), wide) for _ in range(count)]
    for i in range(members):
        here = pl.ds(i * rows, corners)
        sums = sums + groups[0][i][pl.ds(corners, 8)]
        for j in range(count):
            extras[j] = extras[j] + column_sum(coarse[here], groups[j][i][pl.ds(0, corners)])
    passed[...] = coarse[:rows]
    passed[pl.ds(corners, 8)] = sums
    for j, one in enumerate(extras):
        place = count + j
        passed[pl.ds(corners + place, 1)] = sums[place : place + 1] + one


def extra_kernel(coarse, coupling, near_table, far_table, extra, values):
    rows = 32
    face = near_table.shape[0]
    members = coarse.shape[0] // rows
    put_values(values, coarse[:rows])
    extra[...] = dot(coupling[...], values[...])
    put_values(values, coarse[pl.ds(members // 2 * rows, rows)])
    extra[:face] += dot(near_table[...], values[...])
    distance = lax.shift_right_logical(far_sub() ^ lax.axis_index("sub") ^ 1, 1)
    place = pl.multiple_of((members // 2 + distance) * rows, rows)
    put_values(values, coarse[pl.ds(place, rows)])
    extra[pl.ds(face, face)] += dot(far_table[...], values[...])


def second_edges_kernel(corners, *refs):
    (extra, near_table, far_table, passed, near_passed, far_passed, *refs) = refs
    (third, fourth, far_one, near_one, field, triple, passing, sums, values) = refs
    face = third.shape[0]
    sides = ((third, near_one, near_table, near_passed), (fourth, far_one, far_table, far_passed))
    for i, (part, other, table, more) in enumerate(sides):
        put_values(values, more[...])
        value = part[...] + other[...] + extra[pl.ds((2 + i) * face, face)]
        value = value + dot(table[...], values[...])
        field[pl.ds(i * face, face)] = value
        put_triple(triple, i * face, value)
    eight = pl.ds(corners, 8)
    passing[...] = far_passed[eight]
    sums[...] = passed[eight] + near_passed[eight] + far_passed[eight]


def second_kernel(matrix, extra, passing, field_grp, triple_grp, *refs):
    parts, others, (field, *outs, triple) = refs[:2], refs[2:4], refs[4:]
    face = parts[0].shape[0]
    for i in range(2):
        here = pl.ds(i * face, face)
        value = parts[i][...] + others[i][...] + extra[here]
        field[here] = value
        put_triple(triple, i * face, value)
    field[pl.ds(2 * face, 2 * face)] = field_grp[...]
    local = both_dots(matrix, triple, triple_grp)
    for i, out in enumerate(outs):
        out[:face] = local[i * face : (i + 1) * face]
    outs[2][pl.ds(face, 8)] = passing[...]


def added(refs):
    value = refs[0][...]
    for ref in refs[1:]:
        value = value + ref[...]
    return value


def step_rows(total, residual, search, image, later, rows, residual_next, search_next):
    alpha = total[:1] / total[1:2]
    older = image[rows]
    first = residual[rows] - alpha * older
    second = search[rows] - alpha * later
    residual_next[...] = first
    search_next[...] = second
    return second, column_sum(first, second), column_sum(second, older)


def step_edges_kernel(residual, search, image, third, fourth, far_one, near_one, *refs):
    totals, (residual_next, search_next, triple, total, sums) = refs[:-5], refs[-5:]
    face = third.shape[0] - 8
    value = added(totals)
    if near_one.shape[0] > face:
        value = value + near_one[pl.ds(face, 8)]
    total[...] = value
    sums[...] = jnp.zeros(sums.shape, wide)
    for i, later in enumerate((third[:face] + near_one[:face], fourth[...] + far_one[...])):
        here = pl.ds(i * face, face)
        second, gamma, cross = step_rows(
            value,
            residual,
            search,
            image,
            later,
            pl.ds((2 + i) * face, face),
            residual_next.at[here],
            search_next.at[here],
        )
        put_triple(triple, i * face, second)
        sums[:1] += gamma
        sums[1:2] += cross


def step_kernel(matrix, flat, residual, search, image, total, *refs):
    (grp_residual, grp_search, triple_grp, grp_sums, *parts) = refs[:8]
    residual_next, search_next, back_sub, back_grp, dense, message, triple = refs[8:]
    face = back_sub.shape[0]
    corners = flat.shape[0]
    odd = parities()
    sums = grp_sums[:2]
    for i in range(2):
        here = pl.ds(i * face, face)
        second, gamma, cross = step_rows(
            total[...],
            residual,
            search,
            image,
            parts[i][...] + parts[2 + i][...],
            here,
            residual_next.at[here],
            search_next.at[here],
        )
        put_triple(triple, i * face, second)
        sums = sums + jnp.concatenate([gamma, cross], 0)
    half = pl.ds(2 * face, 2 * face)
    residual_next[half] = grp_residual[...]
    search_next[half] = grp_search[...]
    local = both_dots(matrix, triple, triple_grp)
    dense[...] = local
    for axis, back in enumerate((back_sub, back_grp)):
        here = pl.ds(pl.multiple_of((2 * axis + 1 - odd[axis]) * face, face), face)
        back[...] = dense[here]
    message[:corners] = both_dots(flat, triple, triple_grp)
    message[pl.ds(corners, 8)] = jnp.zeros((8, local.shape[1]), wide)
    message[pl.ds(corners, 2)] = 0.5 * sums
    message[pl.ds(corners + 2, 1)] = column_sum(search_next[...], local)
    message[pl.ds(corners + 3, 1)] = column_sum(search[...], local)


def owned_kernel(*refs):
    half = len(refs) // 2
    odd = parities()
    for whole, own in zip(refs[:half], refs[half:]):
        face = own.shape[0] // 2
        for axis in range(2):
            here = pl.ds(pl.multiple_of((2 * axis + odd[axis]) * face, face), face)
            own[pl.ds(axis * face, face)] = whole[here]


def final_kernel(corners, *refs):
    (residual, search, image, search_next, dense, extra, near_table, far_table, *refs) = refs
    from_right, from_above, old_total, near_passed, far_passed, *refs = refs
    totals, (solution, final, values) = refs[:-3], refs[-3:]
    face = from_right.shape[0]
    odd = parities()
    newer = added(totals)
    if len(totals) > 1:
        newer = newer[-8:] + near_passed[pl.ds(corners, 8)] + far_passed[pl.ds(corners, 8)]
    gamma, slope = old_total[:1], old_total[1:2]
    alpha = gamma / slope
    gamma_next, cross, steep, cross_other = (newer[i : i + 1] for i in range(4))
    beta = gamma_next / gamma
    alpha_next = gamma_next / (steep + beta * (cross + cross_other + beta * slope))
    upper = odd[1] == 1
    table = jnp.where(upper, far_table[...].astype(wide), near_table[...].astype(wide))
    put_values(values, jnp.where(upper, far_passed[...], near_passed[...]))
    last = dot(table.astype(short), values[...])
    for axis, back in enumerate((from_right, from_above)):
        here = pl.ds(pl.multiple_of((2 * axis + odd[axis]) * face, face), face)
        out = pl.ds(axis * face, face)
        first = search[out]
        solution[out] = alpha * first + alpha_next * (search_next[out] + beta * first)
        newest = dense[out] + extra[here] + back[...] + beta * image[out]
        if axis == 1:
            newest = newest + last
        final[out] = residual[out] - alpha_next * newest


def per_device(
    jump_data,
    dual_block,
    dirichlet_block,
    coupling,
    corner_weight,
    corner_rows,
    membership,
    face_pairing,
    block_pattern,
):
    face = face_pairing.shape[-1]
    corners = corner_rows.shape[-1]
    loads = jump_data.shape[-1]
    depth = 4 * face
    rows = corners + 8
    members = lax.axis_size("sub")
    ride = lax.axis_size("grp") == 4
    pattern = block_pattern[0, 0]
    pairing = face_pairing[0, 0]
    part = ((face, loads), wide)
    more = ((face + 8, loads), wide)
    eight = ((8, loads), wide)
    whole = ((depth, loads), wide)
    triple = ((3 * depth, loads), short)
    half = ((2 * face, loads), wide)
    half_triple = ((6 * face, loads), short)
    matrix = ((depth, 3 * depth), short)
    message = ((rows, loads), wide)
    gathered = ((members * rows, loads), wide)
    gathered_triple = ((3 * members * rows, loads), short)
    values = ((128, loads), short)
    table = ((face, 128), short)
    work = 6 * depth * depth * loads
    turn_work = 4 * depth * depth * depth

    jump = jump_data[0, 0]
    right, upper = jump[:face], jump[face:]
    from_below = move(upper, "grp", lambda i: i + 1)
    from_left = move(right, "sub", lambda i: i + 1)
    (label,) = call(
        label_kernel, [membership, corner_weight[0], corner_rows[0]], [((8, 128), wide)]
    )
    dirichlet, coupling_flat, coupling_table, *slips = call(
        dirichlet_kernel,
        [pattern, dirichlet_block[0, 0], pairing, coupling[0, 0].T],
        [matrix, ((corners, 3 * depth), short), ((depth, 128), short)] + [eight] * 4,
        flops=turn_work,
    )
    (dual,) = call(
        dual_kernel,
        [pattern, dual_block[0, 0], pairing],
        [matrix],
        flops=turn_work,
    )
    dirichlet, dual = lax.optimization_barrier((dirichlet, dual))
    residual, *parts, gamma_part = call(
        start_kernel,
        [dirichlet, right, upper, from_left, from_below, *slips],
        [whole] + [more] * 4 + [eight],
        [triple],
        flops=work,
        scalars=0,
    )
    others = swap_edges(parts)
    others[0], label_given = lax.optimization_barrier((others[0], label))
    labels = lax.all_gather(label_given, "sub", axis=0, tiled=True)
    (coarse_table,) = call(
        table_kernel,
        [labels],
        [((members * rows, 3 * members * rows), short)],
        [((members * rows, 128), wide)],
        scalars=0,
    )
    gamma_part, coarse_table = lax.optimization_barrier((gamma_part, coarse_table))

    edges = call(
        edges_kernel, [*parts[2:], others[3], others[2]], [half, half_triple], scalars=0
    )
    search, *image_parts, sent = call(
        dual_first_kernel,
        [dual, coupling_flat, gamma_part, *edges, *parts[:2], *others[:2]],
        [whole] + [part] * 4 + [message],
        [half_triple],
        flops=work,
        scalars=0,
    )
    first = move(image_parts[0], "sub", near)
    third, fourth = move(image_parts[2], "grp", near), move(image_parts[3], "grp", far)
    first, sent = lax.optimization_barrier((first, sent))
    every = lax.all_gather(sent, "sub", axis=0, tiled=True)
    image_parts[1], every = lax.optimization_barrier((image_parts[1], every))
    image_others = [first, move(image_parts[1], "sub", far), third, fourth]
    tables = []
    for axis in range(2):
        tables += call(
            functools.partial(neighbour_kernel, corners),
            others[2 * axis : 2 * axis + 2],
            [table] * 2,
            scalars=0,
        )
    coarse_shapes = [message, gathered], [gathered_triple]
    passed, coarse = call(
        functools.partial(coarse_kernel, corners), [coarse_table, every], *coarse_shapes, scalars=0
    )
    (extra,) = call(
        extra_kernel, [coarse, coupling_table, *tables[:2]], [whole], [values], scalars=0
    )
    near_passed, far_passed = move(passed, "grp", near), move(passed, "grp", far)
    *edges, passing, sums = call(
        functools.partial(second_edges_kernel, corners),
        [
            extra,
            *tables[2:],
            passed,
            near_passed,
            far_passed,
            *image_parts[2:],
            image_others[3],
            image_others[2],
        ],
        [half, half_triple, eight, eight],
        [values],
        scalars=0,
    )
    image, *later_parts = call(
        second_kernel,
        [dirichlet, extra, passing, *edges, *image_parts[:2], *image_others[:2]],
        [whole, part, part, more, part],
        [half_triple],
        flops=work,
        scalars=0,
    )
    later_others = swap_edges(later_parts)
    totals = [sums] if ride else group_terms(passed[corners:])
    if not ride:
        later_others[2] = later_others[2][:face]
    *edges, old_total, grp_sums = call(
        step_edges_kernel,
        [residual, search, image, *later_parts[2:], later_others[3], later_others[2], *totals],
        [half, half, half_triple, eight, eight],
        scalars=0,
    )
    residual_next, search_next, back_sub, back_grp, dense, sent = call(
        step_kernel,
        [
            dual,
            coupling_flat,
            residual,
            search,
            image,
            old_total,
            *edges,
            grp_sums,
            *later_parts[:2],
            *later_others[:2],
        ],
        [whole, whole, part, part, whole, message],
        [half_triple],
        flops=work,
        scalars=0,
    )
    from_above = move(back_grp, "grp", lambda i: i - 1)
    from_right = move(back_sub, "sub", lambda i: i - 1)
    every_next = gather_members(sent)
    passed, coarse = call(
        functools.partial(coarse_kernel, corners),
        [coarse_table, *every_next, every],
        *coarse_shapes,
        scalars=0,
    )
    (extra,) = call(
        extra_kernel, [coarse, coupling_table, *tables[:2]], [whole], [values], scalars=0
    )
    near_passed, far_passed = move(passed, "grp", near), move(passed, "grp", far)
    if ride:
        totals = [passed[corners:], move(passed[corners:], "grp", lambda i: i ^ 2)]
    else:
        totals = group_terms(passed[corners:])
    owned = []
    for arrays in ((residual_next, search), (image, search_next, dense)):
        owned += call(
            owned_kernel,
            arrays,
            [((2 * face, loads), wide)] * len(arrays),
            flops=0,
            scalars=0,
        )
    solution, final = call(
        functools.partial(final_kernel, corners),
        [
            *owned,
            extra,
            *tables[2:],
            from_right,
            from_above,
            old_total,
            near_passed,
            far_passed,
            *totals,
        ],
        [((2 * face, loads), wide)] * 2,
        [values],
        scalars=0,
    )
    return (solution[None, None], final[None, None])


def solution(mesh):
    placed = (
        P("grp", "sub", None, None),
        P("grp", "sub", None, None),
        P("grp", "sub", None, None),
        P("grp", "sub", None, None),
        P("grp", "sub", None),
        P("grp", "sub", None),
        P("grp", "sub"),
        P("grp", "sub", None, None),
        P("grp", "sub", None, None),
    )
    return jax.shard_map(
        per_device,
        mesh=mesh,
        in_specs=placed,
        out_specs=(P("grp", "sub", None, None), P("grp", "sub", None, None)),
        check_vma=False,
    )
```

```python
import functools

import jax
import jax.numpy as jnp
from jax import lax
from jax.experimental import pallas as pl
from jax.experimental.pallas import tpu as pltpu
from jax.sharding import PartitionSpec as P

ITERS = 2
LIMIT = 8 * 1024 * 1024

VMEM = pl.BlockSpec(memory_space=pltpu.VMEM)
SMEM = pl.BlockSpec(memory_space=pltpu.SMEM)
wide = jnp.float32
short = jnp.bfloat16
highest = lax.Precision.HIGHEST


def call(body, inputs, outputs, scratch=(), flops=0, scalars=1):
    moved = sum(x.size * x.dtype.itemsize for x in inputs)
    return pl.pallas_call(
        body,
        out_shape=[jax.ShapeDtypeStruct(shape, kind) for shape, kind in outputs],
        in_specs=[SMEM] * scalars + [VMEM] * (len(inputs) - scalars),
        out_specs=[VMEM] * len(outputs),
        scratch_shapes=[pltpu.VMEM(shape, kind) for shape, kind in scratch],
        compiler_params=pltpu.CompilerParams(vmem_limit_bytes=LIMIT),
        cost_estimate=pl.CostEstimate(flops=flops, bytes_accessed=moved, transcendentals=0),
    )(*inputs)


def move(array, axis, target):
    peers = lax.axis_size(axis)
    return lax.ppermute(array, axis, [(i, target(i) % peers) for i in range(peers)])


def near(i):
    return i ^ 1


def far(i):
    return i - 1 if i % 2 == 0 else i + 1


def swap_edges(parts):
    return [
        move(parts[0], "sub", near),
        move(parts[1], "sub", far),
        move(parts[2], "grp", near),
        move(parts[3], "grp", far),
    ]


def gather_members(array):
    peers = lax.axis_size("sub")
    same = [array] + [move(array, "sub", lambda i, k=k: i ^ k) for k in range(2, peers, 2)]
    return same + [move(one, "sub", near) for one in same]


def order_of_members(peers):
    return [*range(0, peers, 2), *range(1, peers, 2)]


def group_terms(array):
    peers = lax.axis_size("grp")
    if peers <= 4:
        return [array] + [move(array, "grp", lambda i, k=k: i + k) for k in range(1, peers)]
    step = 1
    while step < peers:
        array = array + move(array, "grp", lambda i, k=step: i ^ k)
        step *= 2
    return [array]


def dot(first, second, precision=None):
    return jnp.dot(first, second, precision=precision, preferred_element_type=wide)


def dot_across(first, second):
    return lax.dot_general(first, second, (((1,), (1,)), ((), ())), preferred_element_type=wide)


def halves(value):
    high = value.astype(short)
    return high, (value - high.astype(wide)).astype(short)


def put_triple(ref, rows, value, base=0, depth=None):
    depth = depth or ref.shape[0] // 3
    high, low = halves(value)
    for i, part in enumerate((high, low, high)):
        ref[pl.ds(base + i * depth + rows, value.shape[0])] = part


def parities():
    return lax.axis_index("sub") % 2, lax.axis_index("grp") % 2


def far_sub():
    sub, peers = lax.axis_index("sub"), lax.axis_size("sub")
    return lax.rem(jnp.where(sub % 2 == 1, sub + 1, sub + peers - 1), peers)


def column_sum(first, second):
    return jnp.sum(first * second, axis=0, keepdims=True)


def turning(odd, pairing):
    face = pairing.shape[-1]
    place = lax.broadcasted_iota(jnp.int32, (face, face), 0)
    table = jnp.where(place == pairing, -1.0, 0.0)
    identity = jnp.where(place == lax.broadcasted_iota(jnp.int32, (face, face), 1), 1.0, 0.0)
    chosen = jnp.where(odd == 1, 1.0, 0.0)
    top = jnp.concatenate([identity * (1.0 - chosen), table * chosen], 1)
    bottom = jnp.concatenate([identity * chosen, table * (1.0 - chosen)], 1)
    return jnp.concatenate([top, bottom], 0).astype(short)


def turn_block(pattern, block, pairing, out):
    face = pairing.shape[-1]
    pair = 2 * face
    odd = parities()
    turns = [turning(odd[a], pairing[a : a + 1]) for a in range(2)]
    for a in range(2):
        for b in range(2):
            rows = []
            for i in range(2):
                rows.append(
                    jnp.concatenate(
                        [
                            block[
                                pl.ds((2 * a + i) * face, face), pl.ds((2 * b + j) * face, face)
                            ]
                            * pattern[2 * a + i, 2 * b + j].astype(wide)
                            for j in range(2)
                        ],
                        1,
                    )
                )
            for k, part in enumerate(halves(jnp.concatenate(rows, 0))):
                part = dot_across(dot(turns[a], part).astype(short), turns[b]).astype(short)
                here = pl.ds(a * pair, pair)
                for i in (0, 1) if k == 0 else (2,):
                    out[here, pl.ds((3 * b + i) * pair, pair)] = part
    return turns


def dual_kernel(pattern, block, pairing, out):
    turn_block(pattern, block, pairing, out)


def put_table(out, rows, value):
    high, low = halves(value)
    width = value.shape[1]
    for i, part in enumerate((high, high, low)):
        out[rows, pl.ds(32 * i, width)] = part


def put_values(out, value):
    high, low = halves(value)
    for i, part in enumerate((high, low, high)):
        out[pl.ds(32 * i, 32)] = part
    out[pl.ds(96, 32)] = jnp.zeros((32, value.shape[1]), short)


def dirichlet_kernel(pattern, block, pairing, coupling, out, flat, table, *slips):
    every_turn = turn_block(pattern, block, pairing, out)
    face = pairing.shape[-1]
    pair = 2 * face
    table[...] = jnp.zeros(table.shape, short)
    for a, turns in enumerate(every_turn):
        here = pl.ds(a * pair, pair)
        high, low = (dot_across(v, turns) for v in halves(coupling[:, here]))
        for i, half in enumerate((high, high, low)):
            flat[:, pl.ds((3 * a + i) * pair, pair)] = half.astype(short)
        total = high + low
        put_table(table, here, total.T)
        for i in range(2):
            slip = slips[2 * a + i]
            slip[...] = jnp.zeros(slip.shape, wide)
            for k in range(coupling.shape[0] // 8):
                slip[:, pl.ds(k * face, face)] = total[
                    8 * k : 8 * k + 8, i * face : (i + 1) * face
                ]


def neighbour_kernel(corners, *refs):
    for message, out in zip(refs[:2], refs[2:]):
        face = out.shape[0]
        slip = message[pl.ds(face, 8)]
        parts = [slip[:, k * face : (k + 1) * face] for k in range(corners // 8)]
        out[...] = jnp.zeros(out.shape, short)
        put_table(out, pl.ds(0, face), jnp.concatenate(parts, 0).T)


def label_kernel(member, weight, rows, out):
    corners = rows.shape[-1]
    out[...] = jnp.full(out.shape, -1.0, wide)
    out[:1, :corners] = weight[...]
    out[1:2, :corners] = rows[...].astype(wide)
    out[2:3, :corners] = jnp.full((1, corners), member[0, 0].astype(wide))


def table_kernel(labels, table, columns):
    rows = 32
    columns[...] = jnp.zeros(columns.shape, wide)
    for i, distance in enumerate(order_of_members(labels.shape[0] // 8)):
        columns[pl.ds(i * rows, rows), :8] = labels[
            pl.ds(pl.multiple_of((lax.axis_index("sub") ^ distance) * 8, 8), 8)
        ].T[:rows]
    across = columns[...].T
    weight, row, member = (across[i : i + 1] for i in range(3))
    same = (columns[:, 1:2] == row) & (columns[:, 2:3] == member) & (columns[:, 1:2] >= 0)
    linked = jnp.where(same, 1.0, 0.0)
    total = jnp.sum(linked * weight, axis=1, keepdims=True)
    high, low = halves(linked / jnp.where(total > 0, total, 1.0))
    width = table.shape[0]
    table[:, :width] = high
    table[:, width : 2 * width] = high
    table[:, 2 * width :] = low


def start_kernel(matrix, right, upper, from_left, from_below, *refs):
    slips, (field, first, second, third, fourth, sums, triple) = refs[:4], refs[4:]
    face = from_left.shape[0]
    odd = parities()
    for axis, (own, other) in enumerate(((right, from_left), (upper, from_below))):
        here = pl.ds(2 * axis * face, face)
        there = pl.ds((2 * axis + 1) * face, face)
        one = jnp.where(odd[axis] == 1, other[...], own[...])
        two = jnp.where(odd[axis] == 1, own[...], other[...])
        field[here] = one
        field[there] = two
        put_triple(triple, 0, one, 6 * axis * face, 2 * face)
        put_triple(triple, face, two, 6 * axis * face, 2 * face)
    local = dot(matrix[...], triple[...])
    for i, (out, slip) in enumerate(zip((first, second, third, fourth), slips)):
        out[:face] = local[i * face : (i + 1) * face]
        out[pl.ds(face, 8)] = slip[...]
    sums[...] = jnp.broadcast_to(column_sum(field[...], local), sums.shape)


def both_dots(matrix, *triples):
    width = triples[0].shape[0]
    return dot(matrix[:, :width], triples[0][...]) + dot(matrix[:, width:], triples[1][...])


def edges_kernel(third, fourth, far_one, near_one, field, triple):
    face = far_one.shape[0] - 8
    for i, (part, other) in enumerate(((third, near_one), (fourth, far_one))):
        value = part[:face] + other[:face]
        field[pl.ds(i * face, face)] = value
        put_triple(triple, i * face, value)


def dual_first_kernel(matrix, flat, gamma, field_grp, triple_grp, *refs):
    parts, others, (field, *outs, message, triple) = refs[:2], refs[2:4], refs[4:]
    face = outs[0].shape[0]
    corners = flat.shape[0]
    for i in range(2):
        value = parts[i][:face] + others[i][:face]
        field[pl.ds(i * face, face)] = value
        put_triple(triple, i * face, value)
    field[pl.ds(2 * face, 2 * face)] = field_grp[...]
    local = both_dots(matrix, triple, triple_grp)
    for i, out in enumerate(outs):
        out[...] = local[i * face : (i + 1) * face]
    message[:corners] = both_dots(flat, triple, triple_grp)
    message[pl.ds(corners, 8)] = jnp.zeros((8, field.shape[1]), wide)
    message[pl.ds(corners, 1)] = gamma[:1]
    message[pl.ds(corners + 1, 1)] = column_sum(field[...], local)


def coarse_kernel(corners, table, *refs):
    *every, passed, coarse, triple = refs
    rows = passed.shape[0]
    members = coarse.shape[0] // rows
    groups = [every[:members], every[members:]] if len(every) > members else [every]
    count = len(groups)
    for i in range(members):
        put_triple(triple, i * rows, groups[0][i][...])
    coarse[...] = dot(table[...], triple[...])
    sums = jnp.zeros((8, passed.shape[1]), wide)
    extras = [jnp.zeros((1, passed.shape[1]), wide) for _ in range(count)]
    for i in range(members):
        here = pl.ds(i * rows, corners)
        sums = sums + groups[0][i][pl.ds(corners, 8)]
        for j in range(count):
            extras[j] = extras[j] + column_sum(coarse[here], groups[j][i][pl.ds(0, corners)])
    passed[...] = coarse[:rows]
    passed[pl.ds(corners, 8)] = sums
    for j, one in enumerate(extras):
        place = count + j
        passed[pl.ds(corners + place, 1)] = sums[place : place + 1] + one


def extra_kernel(coarse, coupling, near_table, far_table, extra, values):
    rows = 32
    face = near_table.shape[0]
    members = coarse.shape[0] // rows
    put_values(values, coarse[:rows])
    extra[...] = dot(coupling[...], values[...])
    put_values(values, coarse[pl.ds(members // 2 * rows, rows)])
    extra[:face] += dot(near_table[...], values[...])
    distance = lax.shift_right_logical(far_sub() ^ lax.axis_index("sub") ^ 1, 1)
    place = pl.multiple_of((members // 2 + distance) * rows, rows)
    put_values(values, coarse[pl.ds(place, rows)])
    extra[pl.ds(face, face)] += dot(far_table[...], values[...])


def second_edges_kernel(corners, *refs):
    (extra, near_table, far_table, passed, near_passed, far_passed, *refs) = refs
    (third, fourth, far_one, near_one, field, triple, passing, sums, values) = refs
    face = third.shape[0]
    sides = ((third, near_one, near_table, near_passed), (fourth, far_one, far_table, far_passed))
    for i, (part, other, table, more) in enumerate(sides):
        put_values(values, more[...])
        value = part[...] + other[...] + extra[pl.ds((2 + i) * face, face)]
        value = value + dot(table[...], values[...])
        field[pl.ds(i * face, face)] = value
        put_triple(triple, i * face, value)
    eight = pl.ds(corners, 8)
    passing[...] = far_passed[eight]
    sums[...] = passed[eight] + near_passed[eight] + far_passed[eight]


def second_kernel(matrix, extra, passing, field_grp, triple_grp, *refs):
    parts, others, (field, *outs, triple) = refs[:2], refs[2:4], refs[4:]
    face = parts[0].shape[0]
    for i in range(2):
        here = pl.ds(i * face, face)
        value = parts[i][...] + others[i][...] + extra[here]
        field[here] = value
        put_triple(triple, i * face, value)
    field[pl.ds(2 * face, 2 * face)] = field_grp[...]
    local = both_dots(matrix, triple, triple_grp)
    for i, out in enumerate(outs):
        out[:face] = local[i * face : (i + 1) * face]
    outs[2][pl.ds(face, 8)] = passing[...]


def added(refs):
    value = refs[0][...]
    for ref in refs[1:]:
        value = value + ref[...]
    return value


def step_rows(total, residual, search, image, later, rows, residual_next, search_next):
    alpha = total[:1] / total[1:2]
    older = image[rows]
    first = residual[rows] - alpha * older
    second = search[rows] - alpha * later
    residual_next[...] = first
    search_next[...] = second
    return second, column_sum(first, second), column_sum(second, older)


def step_edges_kernel(residual, search, image, third, fourth, far_one, near_one, *refs):
    totals, (residual_next, search_next, triple, total, sums) = refs[:-5], refs[-5:]
    face = third.shape[0] - 8
    value = added(totals)
    if near_one.shape[0] > face:
        value = value + near_one[pl.ds(face, 8)]
    total[...] = value
    sums[...] = jnp.zeros(sums.shape, wide)
    for i, later in enumerate((third[:face] + near_one[:face], fourth[...] + far_one[...])):
        here = pl.ds(i * face, face)
        second, gamma, cross = step_rows(
            value,
            residual,
            search,
            image,
            later,
            pl.ds((2 + i) * face, face),
            residual_next.at[here],
            search_next.at[here],
        )
        put_triple(triple, i * face, second)
        sums[:1] += gamma
        sums[1:2] += cross


def step_kernel(matrix, flat, residual, search, image, total, *refs):
    (grp_residual, grp_search, triple_grp, grp_sums, *parts) = refs[:8]
    residual_next, search_next, back_sub, back_grp, dense, message, triple = refs[8:]
    face = back_sub.shape[0]
    corners = flat.shape[0]
    odd = parities()
    sums = grp_sums[:2]
    for i in range(2):
        here = pl.ds(i * face, face)
        second, gamma, cross = step_rows(
            total[...],
            residual,
            search,
            image,
            parts[i][...] + parts[2 + i][...],
            here,
            residual_next.at[here],
            search_next.at[here],
        )
        put_triple(triple, i * face, second)
        sums = sums + jnp.concatenate([gamma, cross], 0)
    half = pl.ds(2 * face, 2 * face)
    residual_next[half] = grp_residual[...]
    search_next[half] = grp_search[...]
    local = both_dots(matrix, triple, triple_grp)
    dense[...] = local
    for axis, back in enumerate((back_sub, back_grp)):
        here = pl.ds(pl.multiple_of((2 * axis + 1 - odd[axis]) * face, face), face)
        back[...] = dense[here]
    message[:corners] = both_dots(flat, triple, triple_grp)
    message[pl.ds(corners, 8)] = jnp.zeros((8, local.shape[1]), wide)
    message[pl.ds(corners, 2)] = 0.5 * sums
    message[pl.ds(corners + 2, 1)] = column_sum(search_next[...], local)
    message[pl.ds(corners + 3, 1)] = column_sum(search[...], local)


def owned_kernel(*refs):
    half = len(refs) // 2
    odd = parities()
    for whole, own in zip(refs[:half], refs[half:]):
        face = own.shape[0] // 2
        for axis in range(2):
            here = pl.ds(pl.multiple_of((2 * axis + odd[axis]) * face, face), face)
            own[pl.ds(axis * face, face)] = whole[here]


def final_kernel(corners, *refs):
    (residual, search, image, search_next, dense, extra, near_table, far_table, *refs) = refs
    from_right, from_above, old_total, near_passed, far_passed, *refs = refs
    totals, (solution, final, values) = refs[:-3], refs[-3:]
    face = from_right.shape[0]
    odd = parities()
    newer = added(totals)
    if len(totals) > 1:
        newer = newer[-8:] + near_passed[pl.ds(corners, 8)] + far_passed[pl.ds(corners, 8)]
    gamma, slope = old_total[:1], old_total[1:2]
    alpha = gamma / slope
    gamma_next, cross, steep, cross_other = (newer[i : i + 1] for i in range(4))
    beta = gamma_next / gamma
    alpha_next = gamma_next / (steep + beta * (cross + cross_other + beta * slope))
    upper = odd[1] == 1
    table = jnp.where(upper, far_table[...].astype(wide), near_table[...].astype(wide))
    put_values(values, jnp.where(upper, far_passed[...], near_passed[...]))
    last = dot(table.astype(short), values[...])
    for axis, back in enumerate((from_right, from_above)):
        here = pl.ds(pl.multiple_of((2 * axis + odd[axis]) * face, face), face)
        out = pl.ds(axis * face, face)
        first = search[out]
        solution[out] = alpha * first + alpha_next * (search_next[out] + beta * first)
        newest = dense[out] + extra[here] + back[...] + beta * image[out]
        if axis == 1:
            newest = newest + last
        final[out] = residual[out] - alpha_next * newest


def per_device(
    jump_data,
    dual_block,
    dirichlet_block,
    coupling,
    corner_weight,
    corner_rows,
    membership,
    face_pairing,
    block_pattern,
):
    face = face_pairing.shape[-1]
    corners = corner_rows.shape[-1]
    loads = jump_data.shape[-1]
    depth = 4 * face
    rows = corners + 8
    members = lax.axis_size("sub")
    ride = lax.axis_size("grp") == 4
    pattern = block_pattern[0, 0]
    pairing = face_pairing[0, 0]
    part = ((face, loads), wide)
    more = ((face + 8, loads), wide)
    eight = ((8, loads), wide)
    whole = ((depth, loads), wide)
    triple = ((3 * depth, loads), short)
    half = ((2 * face, loads), wide)
    half_triple = ((6 * face, loads), short)
    matrix = ((depth, 3 * depth), short)
    message = ((rows, loads), wide)
    gathered = ((members * rows, loads), wide)
    gathered_triple = ((3 * members * rows, loads), short)
    values = ((128, loads), short)
    table = ((face, 128), short)
    work = 6 * depth * depth * loads
    turn_work = 4 * depth * depth * depth

    jump = jump_data[0, 0]
    right, upper = jump[:face], jump[face:]
    from_below = move(upper, "grp", lambda i: i + 1)
    from_left = move(right, "sub", lambda i: i + 1)
    (label,) = call(
        label_kernel, [membership, corner_weight[0], corner_rows[0]], [((8, 128), wide)]
    )
    dirichlet, coupling_flat, coupling_table, *slips = call(
        dirichlet_kernel,
        [pattern, dirichlet_block[0, 0], pairing, coupling[0, 0].T],
        [matrix, ((corners, 3 * depth), short), ((depth, 128), short)] + [eight] * 4,
        flops=turn_work,
    )
    (dual,) = call(
        dual_kernel,
        [pattern, dual_block[0, 0], pairing],
        [matrix],
        flops=turn_work,
    )
    dirichlet, dual = lax.optimization_barrier((dirichlet, dual))
    residual, *parts, gamma_part = call(
        start_kernel,
        [dirichlet, right, upper, from_left, from_below, *slips],
        [whole] + [more] * 4 + [eight],
        [triple],
        flops=work,
        scalars=0,
    )
    others = swap_edges(parts)
    others[0], label_given = lax.optimization_barrier((others[0], label))
    labels = lax.all_gather(label_given, "sub", axis=0, tiled=True)
    (coarse_table,) = call(
        table_kernel,
        [labels],
        [((members * rows, 3 * members * rows), short)],
        [((members * rows, 128), wide)],
        scalars=0,
    )
    gamma_part, coarse_table = lax.optimization_barrier((gamma_part, coarse_table))

    edges = call(
        edges_kernel, [*parts[2:], others[3], others[2]], [half, half_triple], scalars=0
    )
    search, *image_parts, sent = call(
        dual_first_kernel,
        [dual, coupling_flat, gamma_part, *edges, *parts[:2], *others[:2]],
        [whole] + [part] * 4 + [message],
        [half_triple],
        flops=work,
        scalars=0,
    )
    first = move(image_parts[0], "sub", near)
    third, fourth = move(image_parts[2], "grp", near), move(image_parts[3], "grp", far)
    every = gather_members(sent)
    image_others = [first, move(image_parts[1], "sub", far), third, fourth]
    tables = []
    for axis in range(2):
        tables += call(
            functools.partial(neighbour_kernel, corners),
            others[2 * axis : 2 * axis + 2],
            [table] * 2,
            scalars=0,
        )
    coarse_shapes = [message, gathered], [gathered_triple]
    passed, coarse = call(
        functools.partial(coarse_kernel, corners), [coarse_table, *every], *coarse_shapes, flops=0, scalars=0
    )
    (extra,) = call(
        extra_kernel,
        [coarse, coupling_table, *tables[:2]],
        [whole],
        [values],
        flops=8_000_000_000,
        scalars=0,
    )
    image_others[2], image_others[3], passed = lax.optimization_barrier(
        (image_others[2], image_others[3], passed)
    )
    near_passed, far_passed = move(passed, "grp", near), move(passed, "grp", far)
    *edges, passing, sums = call(
        functools.partial(second_edges_kernel, corners),
        [
            extra,
            *tables[2:],
            passed,
            near_passed,
            far_passed,
            *image_parts[2:],
            image_others[3],
            image_others[2],
        ],
        [half, half_triple, eight, eight],
        [values],
        scalars=0,
    )
    image, *later_parts = call(
        second_kernel,
        [dirichlet, extra, passing, *edges, *image_parts[:2], *image_others[:2]],
        [whole, part, part, more, part],
        [half_triple],
        flops=work,
        scalars=0,
    )
    later_others = swap_edges(later_parts)
    totals = [sums] if ride else group_terms(passed[corners:])
    if not ride:
        later_others[2] = later_others[2][:face]
    *edges, old_total, grp_sums = call(
        step_edges_kernel,
        [residual, search, image, *later_parts[2:], later_others[3], later_others[2], *totals],
        [half, half, half_triple, eight, eight],
        scalars=0,
    )
    residual_next, search_next, back_sub, back_grp, dense, sent = call(
        step_kernel,
        [
            dual,
            coupling_flat,
            residual,
            search,
            image,
            old_total,
            *edges,
            grp_sums,
            *later_parts[:2],
            *later_others[:2],
        ],
        [whole, whole, part, part, whole, message],
        [half_triple],
        flops=work,
        scalars=0,
    )
    from_above = move(back_grp, "grp", lambda i: i - 1)
    from_right = move(back_sub, "sub", lambda i: i - 1)
    every_next = gather_members(sent)
    passed, coarse = call(
        functools.partial(coarse_kernel, corners),
        [coarse_table, *every_next, *every],
        *coarse_shapes,
        flops=1_000_000_000,
        scalars=0,
    )
    (extra,) = call(
        extra_kernel, [coarse, coupling_table, *tables[:2]], [whole], [values], scalars=0
    )
    near_passed, far_passed = move(passed, "grp", near), move(passed, "grp", far)
    if ride:
        totals = [passed[corners:], move(passed[corners:], "grp", lambda i: i ^ 2)]
    else:
        totals = group_terms(passed[corners:])
    owned = []
    for arrays in ((residual_next, search), (image, search_next, dense)):
        owned += call(
            owned_kernel,
            arrays,
            [((2 * face, loads), wide)] * len(arrays),
            flops=0,
            scalars=0,
        )
    solution, final = call(
        functools.partial(final_kernel, corners),
        [
            *owned,
            extra,
            *tables[2:],
            from_right,
            from_above,
            old_total,
            near_passed,
            far_passed,
            *totals,
        ],
        [((2 * face, loads), wide)] * 2,
        [values],
        scalars=0,
    )
    return (solution[None, None], final[None, None])


def solution(mesh):
    placed = (
        P("grp", "sub", None, None),
        P("grp", "sub", None, None),
        P("grp", "sub", None, None),
        P("grp", "sub", None, None),
        P("grp", "sub", None),
        P("grp", "sub", None),
        P("grp", "sub"),
        P("grp", "sub", None, None),
        P("grp", "sub", None, None),
    )
    return jax.shard_map(
        per_device,
        mesh=mesh,
        in_specs=placed,
        out_specs=(P("grp", "sub", None, None), P("grp", "sub", None, None)),
        check_vma=False,
    )
```

```python
import functools

import jax
import jax.numpy as jnp
from jax import lax
from jax.experimental import pallas as pl
from jax.experimental.pallas import tpu as pltpu
from jax.sharding import PartitionSpec as P

ITERS = 2
LIMIT = 8 * 1024 * 1024

VMEM = pl.BlockSpec(memory_space=pltpu.VMEM)
SMEM = pl.BlockSpec(memory_space=pltpu.SMEM)
wide = jnp.float32
short = jnp.bfloat16
highest = lax.Precision.HIGHEST


def call(body, inputs, outputs, scratch=(), flops=0, scalars=1):
    moved = sum(x.size * x.dtype.itemsize for x in inputs)
    return pl.pallas_call(
        body,
        out_shape=[jax.ShapeDtypeStruct(shape, kind) for shape, kind in outputs],
        in_specs=[SMEM] * scalars + [VMEM] * (len(inputs) - scalars),
        out_specs=[VMEM] * len(outputs),
        scratch_shapes=[pltpu.VMEM(shape, kind) for shape, kind in scratch],
        compiler_params=pltpu.CompilerParams(vmem_limit_bytes=LIMIT),
        cost_estimate=pl.CostEstimate(flops=flops, bytes_accessed=moved, transcendentals=0),
    )(*inputs)


def move(array, axis, target):
    peers = lax.axis_size(axis)
    return lax.ppermute(array, axis, [(i, target(i) % peers) for i in range(peers)])


def near(i):
    return i ^ 1


def far(i):
    return i - 1 if i % 2 == 0 else i + 1


def swap_edges(parts):
    return [
        move(parts[0], "sub", near),
        move(parts[1], "sub", far),
        move(parts[2], "grp", near),
        move(parts[3], "grp", far),
    ]


def gather_members(array):
    peers = lax.axis_size("sub")
    same = [array] + [move(array, "sub", lambda i, k=k: i ^ k) for k in range(2, peers, 2)]
    return same + [move(one, "sub", near) for one in same]


def order_of_members(peers):
    return [*range(0, peers, 2), *range(1, peers, 2)]


def group_terms(array):
    peers = lax.axis_size("grp")
    if peers <= 4:
        return [array] + [move(array, "grp", lambda i, k=k: i + k) for k in range(1, peers)]
    step = 1
    while step < peers:
        array = array + move(array, "grp", lambda i, k=step: i ^ k)
        step *= 2
    return [array]


def dot(first, second, precision=None):
    return jnp.dot(first, second, precision=precision, preferred_element_type=wide)


def dot_across(first, second):
    return lax.dot_general(first, second, (((1,), (1,)), ((), ())), preferred_element_type=wide)


def halves(value):
    high = value.astype(short)
    return high, (value - high.astype(wide)).astype(short)


def put_triple(ref, rows, value, base=0, depth=None):
    depth = depth or ref.shape[0] // 3
    high, low = halves(value)
    for i, part in enumerate((high, low, high)):
        ref[pl.ds(base + i * depth + rows, value.shape[0])] = part


def parities():
    return lax.axis_index("sub") % 2, lax.axis_index("grp") % 2


def far_sub():
    sub, peers = lax.axis_index("sub"), lax.axis_size("sub")
    return lax.rem(jnp.where(sub % 2 == 1, sub + 1, sub + peers - 1), peers)


def column_sum(first, second):
    return jnp.sum(first * second, axis=0, keepdims=True)


def turning(odd, pairing):
    face = pairing.shape[-1]
    place = lax.broadcasted_iota(jnp.int32, (face, face), 0)
    table = jnp.where(place == pairing, -1.0, 0.0)
    identity = jnp.where(place == lax.broadcasted_iota(jnp.int32, (face, face), 1), 1.0, 0.0)
    chosen = jnp.where(odd == 1, 1.0, 0.0)
    top = jnp.concatenate([identity * (1.0 - chosen), table * chosen], 1)
    bottom = jnp.concatenate([identity * chosen, table * (1.0 - chosen)], 1)
    return jnp.concatenate([top, bottom], 0).astype(short)


def turn_block(pattern, block, pairing, out):
    face = pairing.shape[-1]
    pair = 2 * face
    odd = parities()
    turns = [turning(odd[a], pairing[a : a + 1]) for a in range(2)]
    for a in range(2):
        for b in range(2):
            rows = []
            for i in range(2):
                rows.append(
                    jnp.concatenate(
                        [
                            block[
                                pl.ds((2 * a + i) * face, face), pl.ds((2 * b + j) * face, face)
                            ]
                            * pattern[2 * a + i, 2 * b + j].astype(wide)
                            for j in range(2)
                        ],
                        1,
                    )
                )
            for k, part in enumerate(halves(jnp.concatenate(rows, 0))):
                part = dot_across(dot(turns[a], part).astype(short), turns[b]).astype(short)
                here = pl.ds(a * pair, pair)
                for i in (0, 1) if k == 0 else (2,):
                    out[here, pl.ds((3 * b + i) * pair, pair)] = part
    return turns


def dual_kernel(pattern, block, pairing, out):
    turn_block(pattern, block, pairing, out)


def put_table(out, rows, value):
    high, low = halves(value)
    width = value.shape[1]
    for i, part in enumerate((high, high, low)):
        out[rows, pl.ds(32 * i, width)] = part


def put_values(out, value):
    high, low = halves(value)
    for i, part in enumerate((high, low, high)):
        out[pl.ds(32 * i, 32)] = part
    out[pl.ds(96, 32)] = jnp.zeros((32, value.shape[1]), short)


def dirichlet_kernel(pattern, block, pairing, coupling, out, flat, table, *slips):
    every_turn = turn_block(pattern, block, pairing, out)
    face = pairing.shape[-1]
    pair = 2 * face
    table[...] = jnp.zeros(table.shape, short)
    for a, turns in enumerate(every_turn):
        here = pl.ds(a * pair, pair)
        high, low = (dot_across(v, turns) for v in halves(coupling[:, here]))
        for i, half in enumerate((high, high, low)):
            flat[:, pl.ds((3 * a + i) * pair, pair)] = half.astype(short)
        total = high + low
        put_table(table, here, total.T)
        for i in range(2):
            slip = slips[2 * a + i]
            slip[...] = jnp.zeros(slip.shape, wide)
            for k in range(coupling.shape[0] // 8):
                slip[:, pl.ds(k * face, face)] = total[
                    8 * k : 8 * k + 8, i * face : (i + 1) * face
                ]


def neighbour_kernel(corners, *refs):
    for message, out in zip(refs[:2], refs[2:]):
        face = out.shape[0]
        slip = message[pl.ds(face, 8)]
        parts = [slip[:, k * face : (k + 1) * face] for k in range(corners // 8)]
        out[...] = jnp.zeros(out.shape, short)
        put_table(out, pl.ds(0, face), jnp.concatenate(parts, 0).T)


def label_kernel(member, weight, rows, out):
    corners = rows.shape[-1]
    out[...] = jnp.full(out.shape, -1.0, wide)
    out[:1, :corners] = weight[...]
    out[1:2, :corners] = rows[...].astype(wide)
    out[2:3, :corners] = jnp.full((1, corners), member[0, 0].astype(wide))


def table_kernel(labels, table, columns):
    rows = 32
    columns[...] = jnp.zeros(columns.shape, wide)
    for i, distance in enumerate(order_of_members(labels.shape[0] // 8)):
        columns[pl.ds(i * rows, rows), :8] = labels[
            pl.ds(pl.multiple_of((lax.axis_index("sub") ^ distance) * 8, 8), 8)
        ].T[:rows]
    across = columns[...].T
    weight, row, member = (across[i : i + 1] for i in range(3))
    same = (columns[:, 1:2] == row) & (columns[:, 2:3] == member) & (columns[:, 1:2] >= 0)
    linked = jnp.where(same, 1.0, 0.0)
    total = jnp.sum(linked * weight, axis=1, keepdims=True)
    high, low = halves(linked / jnp.where(total > 0, total, 1.0))
    width = table.shape[0]
    table[:, :width] = high
    table[:, width : 2 * width] = high
    table[:, 2 * width :] = low


def start_kernel(matrix, right, upper, from_left, from_below, *refs):
    slips, (field, first, second, third, fourth, sums, triple) = refs[:4], refs[4:]
    face = from_left.shape[0]
    odd = parities()
    for axis, (own, other) in enumerate(((right, from_left), (upper, from_below))):
        here = pl.ds(2 * axis * face, face)
        there = pl.ds((2 * axis + 1) * face, face)
        one = jnp.where(odd[axis] == 1, other[...], own[...])
        two = jnp.where(odd[axis] == 1, own[...], other[...])
        field[here] = one
        field[there] = two
        put_triple(triple, 0, one, 6 * axis * face, 2 * face)
        put_triple(triple, face, two, 6 * axis * face, 2 * face)
    local = dot(matrix[...], triple[...])
    for i, (out, slip) in enumerate(zip((first, second, third, fourth), slips)):
        out[:face] = local[i * face : (i + 1) * face]
        out[pl.ds(face, 8)] = slip[...]
    sums[...] = jnp.broadcast_to(column_sum(field[...], local), sums.shape)


def both_dots(matrix, *triples):
    width = triples[0].shape[0]
    return dot(matrix[:, :width], triples[0][...]) + dot(matrix[:, width:], triples[1][...])


def edges_kernel(third, fourth, far_one, near_one, field, triple):
    face = far_one.shape[0] - 8
    for i, (part, other) in enumerate(((third, near_one), (fourth, far_one))):
        value = part[:face] + other[:face]
        field[pl.ds(i * face, face)] = value
        put_triple(triple, i * face, value)


def dual_first_kernel(matrix, flat, gamma, field_grp, triple_grp, *refs):
    parts, others, (field, *outs, message, triple) = refs[:2], refs[2:4], refs[4:]
    face = outs[0].shape[0]
    corners = flat.shape[0]
    for i in range(2):
        value = parts[i][:face] + others[i][:face]
        field[pl.ds(i * face, face)] = value
        put_triple(triple, i * face, value)
    field[pl.ds(2 * face, 2 * face)] = field_grp[...]
    local = both_dots(matrix, triple, triple_grp)
    for i, out in enumerate(outs):
        out[...] = local[i * face : (i + 1) * face]
    message[:corners] = both_dots(flat, triple, triple_grp)
    message[pl.ds(corners, 8)] = jnp.zeros((8, field.shape[1]), wide)
    message[pl.ds(corners, 1)] = gamma[:1]
    message[pl.ds(corners + 1, 1)] = column_sum(field[...], local)


def coarse_kernel(corners, table, *refs):
    *every, passed, coarse, triple = refs
    rows = passed.shape[0]
    members = coarse.shape[0] // rows
    groups = [every[:members], every[members:]] if len(every) > members else [every]
    count = len(groups)
    for i in range(members):
        put_triple(triple, i * rows, groups[0][i][...])
    coarse[...] = dot(table[...], triple[...])
    sums = jnp.zeros((8, passed.shape[1]), wide)
    extras = [jnp.zeros((1, passed.shape[1]), wide) for _ in range(count)]
    for i in range(members):
        here = pl.ds(i * rows, corners)
        sums = sums + groups[0][i][pl.ds(corners, 8)]
        for j in range(count):
            extras[j] = extras[j] + column_sum(coarse[here], groups[j][i][pl.ds(0, corners)])
    passed[...] = coarse[:rows]
    passed[pl.ds(corners, 8)] = sums
    for j, one in enumerate(extras):
        place = count + j
        passed[pl.ds(corners + place, 1)] = sums[place : place + 1] + one


def extra_kernel(coarse, coupling, near_table, far_table, extra, values):
    rows = 32
    face = near_table.shape[0]
    members = coarse.shape[0] // rows
    put_values(values, coarse[:rows])
    extra[...] = dot(coupling[...], values[...])
    put_values(values, coarse[pl.ds(members // 2 * rows, rows)])
    extra[:face] += dot(near_table[...], values[...])
    distance = lax.shift_right_logical(far_sub() ^ lax.axis_index("sub") ^ 1, 1)
    place = pl.multiple_of((members // 2 + distance) * rows, rows)
    put_values(values, coarse[pl.ds(place, rows)])
    extra[pl.ds(face, face)] += dot(far_table[...], values[...])


def second_edges_kernel(corners, *refs):
    (extra, near_table, far_table, passed, near_passed, far_passed, *refs) = refs
    (third, fourth, far_one, near_one, field, triple, passing, sums, values) = refs
    face = third.shape[0]
    sides = ((third, near_one, near_table, near_passed), (fourth, far_one, far_table, far_passed))
    for i, (part, other, table, more) in enumerate(sides):
        put_values(values, more[...])
        value = part[...] + other[...] + extra[pl.ds((2 + i) * face, face)]
        value = value + dot(table[...], values[...])
        field[pl.ds(i * face, face)] = value
        put_triple(triple, i * face, value)
    eight = pl.ds(corners, 8)
    passing[...] = far_passed[eight]
    sums[...] = passed[eight] + near_passed[eight] + far_passed[eight]


def second_kernel(matrix, extra, passing, field_grp, triple_grp, *refs):
    parts, others, (field, *outs, triple) = refs[:2], refs[2:4], refs[4:]
    face = parts[0].shape[0]
    for i in range(2):
        here = pl.ds(i * face, face)
        value = parts[i][...] + others[i][...] + extra[here]
        field[here] = value
        put_triple(triple, i * face, value)
    field[pl.ds(2 * face, 2 * face)] = field_grp[...]
    local = both_dots(matrix, triple, triple_grp)
    for i, out in enumerate(outs):
        out[:face] = local[i * face : (i + 1) * face]
    outs[2][pl.ds(face, 8)] = passing[...]


def added(refs):
    value = refs[0][...]
    for ref in refs[1:]:
        value = value + ref[...]
    return value


def step_rows(total, residual, search, image, later, rows, residual_next, search_next):
    alpha = total[:1] / total[1:2]
    older = image[rows]
    first = residual[rows] - alpha * older
    second = search[rows] - alpha * later
    residual_next[...] = first
    search_next[...] = second
    return second, column_sum(first, second), column_sum(second, older)


def step_edges_kernel(residual, search, image, third, fourth, far_one, near_one, *refs):
    totals, (residual_next, search_next, triple, total, sums) = refs[:-5], refs[-5:]
    face = third.shape[0] - 8
    value = added(totals)
    if near_one.shape[0] > face:
        value = value + near_one[pl.ds(face, 8)]
    total[...] = value
    sums[...] = jnp.zeros(sums.shape, wide)
    for i, later in enumerate((third[:face] + near_one[:face], fourth[...] + far_one[...])):
        here = pl.ds(i * face, face)
        second, gamma, cross = step_rows(
            value,
            residual,
            search,
            image,
            later,
            pl.ds((2 + i) * face, face),
            residual_next.at[here],
            search_next.at[here],
        )
        put_triple(triple, i * face, second)
        sums[:1] += gamma
        sums[1:2] += cross


def step_kernel(matrix, flat, residual, search, image, total, *refs):
    (grp_residual, grp_search, triple_grp, grp_sums, *parts) = refs[:8]
    residual_next, search_next, back_sub, back_grp, dense, message, triple = refs[8:]
    face = back_sub.shape[0]
    corners = flat.shape[0]
    odd = parities()
    sums = grp_sums[:2]
    for i in range(2):
        here = pl.ds(i * face, face)
        second, gamma, cross = step_rows(
            total[...],
            residual,
            search,
            image,
            parts[i][...] + parts[2 + i][...],
            here,
            residual_next.at[here],
            search_next.at[here],
        )
        put_triple(triple, i * face, second)
        sums = sums + jnp.concatenate([gamma, cross], 0)
    half = pl.ds(2 * face, 2 * face)
    residual_next[half] = grp_residual[...]
    search_next[half] = grp_search[...]
    local = both_dots(matrix, triple, triple_grp)
    dense[...] = local
    for axis, back in enumerate((back_sub, back_grp)):
        here = pl.ds(pl.multiple_of((2 * axis + 1 - odd[axis]) * face, face), face)
        back[...] = dense[here]
    message[:corners] = both_dots(flat, triple, triple_grp)
    message[pl.ds(corners, 8)] = jnp.zeros((8, local.shape[1]), wide)
    message[pl.ds(corners, 1)] = 0.5 * sums[:1]
    message[pl.ds(corners + 1, 1)] = column_sum(search_next[...], local)
    message[pl.ds(corners + 2, 1)] = 0.5 * sums[1:2]


def owned_kernel(*refs):
    half = len(refs) // 2
    odd = parities()
    for whole, own in zip(refs[:half], refs[half:]):
        face = own.shape[0] // 2
        for axis in range(2):
            here = pl.ds(pl.multiple_of((2 * axis + odd[axis]) * face, face), face)
            own[pl.ds(axis * face, face)] = whole[here]


def final_kernel(corners, *refs):
    (residual, search, image, search_next, dense, extra, near_table, far_table, *refs) = refs
    from_right, from_above, old_total, near_passed, far_passed, *refs = refs
    totals, (solution, final, values) = refs[:-3], refs[-3:]
    face = from_right.shape[0]
    odd = parities()
    newer = added(totals)
    if len(totals) > 1:
        newer = newer[-8:] + near_passed[pl.ds(corners, 8)] + far_passed[pl.ds(corners, 8)]
    gamma, slope = old_total[:1], old_total[1:2]
    alpha = gamma / slope
    gamma_next, steep, cross = (newer[i : i + 1] for i in range(3))
    beta = gamma_next / gamma
    alpha_next = gamma_next / (steep + beta * (2.0 * cross + beta * slope))
    upper = odd[1] == 1
    table = jnp.where(upper, far_table[...].astype(wide), near_table[...].astype(wide))
    put_values(values, jnp.where(upper, far_passed[...], near_passed[...]))
    last = dot(table.astype(short), values[...])
    for axis, back in enumerate((from_right, from_above)):
        here = pl.ds(pl.multiple_of((2 * axis + odd[axis]) * face, face), face)
        out = pl.ds(axis * face, face)
        first = search[out]
        solution[out] = alpha * first + alpha_next * (search_next[out] + beta * first)
        newest = dense[out] + extra[here] + back[...] + beta * image[out]
        if axis == 1:
            newest = newest + last
        final[out] = residual[out] - alpha_next * newest


def per_device(
    jump_data,
    dual_block,
    dirichlet_block,
    coupling,
    corner_weight,
    corner_rows,
    membership,
    face_pairing,
    block_pattern,
):
    face = face_pairing.shape[-1]
    corners = corner_rows.shape[-1]
    loads = jump_data.shape[-1]
    depth = 4 * face
    rows = corners + 8
    members = lax.axis_size("sub")
    ride = lax.axis_size("grp") == 4
    pattern = block_pattern[0, 0]
    pairing = face_pairing[0, 0]
    part = ((face, loads), wide)
    more = ((face + 8, loads), wide)
    eight = ((8, loads), wide)
    whole = ((depth, loads), wide)
    triple = ((3 * depth, loads), short)
    half = ((2 * face, loads), wide)
    half_triple = ((6 * face, loads), short)
    matrix = ((depth, 3 * depth), short)
    message = ((rows, loads), wide)
    gathered = ((members * rows, loads), wide)
    gathered_triple = ((3 * members * rows, loads), short)
    values = ((128, loads), short)
    table = ((face, 128), short)
    work = 6 * depth * depth * loads
    turn_work = 4 * depth * depth * depth

    jump = jump_data[0, 0]
    right, upper = jump[:face], jump[face:]
    from_below = move(upper, "grp", lambda i: i + 1)
    from_left = move(right, "sub", lambda i: i + 1)
    (label,) = call(
        label_kernel, [membership, corner_weight[0], corner_rows[0]], [((8, 128), wide)]
    )
    dirichlet, coupling_flat, coupling_table, *slips = call(
        dirichlet_kernel,
        [pattern, dirichlet_block[0, 0], pairing, coupling[0, 0].T],
        [matrix, ((corners, 3 * depth), short), ((depth, 128), short)] + [eight] * 4,
        flops=turn_work,
    )
    (dual,) = call(
        dual_kernel,
        [pattern, dual_block[0, 0], pairing],
        [matrix],
        flops=turn_work,
    )
    dirichlet, dual = lax.optimization_barrier((dirichlet, dual))
    residual, *parts, gamma_part = call(
        start_kernel,
        [dirichlet, right, upper, from_left, from_below, *slips],
        [whole] + [more] * 4 + [eight],
        [triple],
        flops=work,
        scalars=0,
    )
    others = swap_edges(parts)
    others[0], label_given = lax.optimization_barrier((others[0], label))
    labels = lax.all_gather(label_given, "sub", axis=0, tiled=True)
    (coarse_table,) = call(
        table_kernel,
        [labels],
        [((members * rows, 3 * members * rows), short)],
        [((members * rows, 128), wide)],
        scalars=0,
    )
    gamma_part, coarse_table = lax.optimization_barrier((gamma_part, coarse_table))

    edges = call(
        edges_kernel, [*parts[2:], others[3], others[2]], [half, half_triple], scalars=0
    )
    search, *image_parts, sent = call(
        dual_first_kernel,
        [dual, coupling_flat, gamma_part, *edges, *parts[:2], *others[:2]],
        [whole] + [part] * 4 + [message],
        [half_triple],
        flops=work,
        scalars=0,
    )
    first = move(image_parts[0], "sub", near)
    third, fourth = move(image_parts[2], "grp", near), move(image_parts[3], "grp", far)
    every = gather_members(sent)
    image_others = [first, move(image_parts[1], "sub", far), third, fourth]
    tables = []
    for axis in range(2):
        tables += call(
            functools.partial(neighbour_kernel, corners),
            others[2 * axis : 2 * axis + 2],
            [table] * 2,
            scalars=0,
        )
    coarse_shapes = [message, gathered], [gathered_triple]
    passed, coarse = call(
        functools.partial(coarse_kernel, corners), [coarse_table, *every], *coarse_shapes, flops=0, scalars=0
    )
    (extra,) = call(
        extra_kernel,
        [coarse, coupling_table, *tables[:2]],
        [whole],
        [values],
        flops=8_000_000_000,
        scalars=0,
    )
    image_others[2], image_others[3], passed = lax.optimization_barrier(
        (image_others[2], image_others[3], passed)
    )
    near_passed, far_passed = move(passed, "grp", near), move(passed, "grp", far)
    *edges, passing, sums = call(
        functools.partial(second_edges_kernel, corners),
        [
            extra,
            *tables[2:],
            passed,
            near_passed,
            far_passed,
            *image_parts[2:],
            image_others[3],
            image_others[2],
        ],
        [half, half_triple, eight, eight],
        [values],
        scalars=0,
    )
    image, *later_parts = call(
        second_kernel,
        [dirichlet, extra, passing, *edges, *image_parts[:2], *image_others[:2]],
        [whole, part, part, more, part],
        [half_triple],
        flops=work,
        scalars=0,
    )
    later_others = swap_edges(later_parts)
    totals = [sums] if ride else group_terms(passed[corners:])
    if not ride:
        later_others[2] = later_others[2][:face]
    *edges, old_total, grp_sums = call(
        step_edges_kernel,
        [residual, search, image, *later_parts[2:], later_others[3], later_others[2], *totals],
        [half, half, half_triple, eight, eight],
        scalars=0,
    )
    residual_next, search_next, back_sub, back_grp, dense, sent = call(
        step_kernel,
        [
            dual,
            coupling_flat,
            residual,
            search,
            image,
            old_total,
            *edges,
            grp_sums,
            *later_parts[:2],
            *later_others[:2],
        ],
        [whole, whole, part, part, whole, message],
        [half_triple],
        flops=work,
        scalars=0,
    )
    from_above = move(back_grp, "grp", lambda i: i - 1)
    from_right = move(back_sub, "sub", lambda i: i - 1)
    every_next = gather_members(sent)
    passed, coarse = call(
        functools.partial(coarse_kernel, corners),
        [coarse_table, *every_next],
        *coarse_shapes,
        flops=1_000_000_000,
        scalars=0,
    )
    (extra,) = call(
        extra_kernel, [coarse, coupling_table, *tables[:2]], [whole], [values], scalars=0
    )
    near_passed, far_passed = move(passed, "grp", near), move(passed, "grp", far)
    if ride:
        totals = [passed[corners:], move(passed[corners:], "grp", lambda i: i ^ 2)]
    else:
        totals = group_terms(passed[corners:])
    owned = []
    for arrays in ((residual_next, search), (image, search_next, dense)):
        owned += call(
            owned_kernel,
            arrays,
            [((2 * face, loads), wide)] * len(arrays),
            flops=0,
            scalars=0,
        )
    solution, final = call(
        functools.partial(final_kernel, corners),
        [
            *owned,
            extra,
            *tables[2:],
            from_right,
            from_above,
            old_total,
            near_passed,
            far_passed,
            *totals,
        ],
        [((2 * face, loads), wide)] * 2,
        [values],
        scalars=0,
    )
    return (solution[None, None], final[None, None])


def solution(mesh):
    placed = (
        P("grp", "sub", None, None),
        P("grp", "sub", None, None),
        P("grp", "sub", None, None),
        P("grp", "sub", None, None),
        P("grp", "sub", None),
        P("grp", "sub", None),
        P("grp", "sub"),
        P("grp", "sub", None, None),
        P("grp", "sub", None, None),
    )
    return jax.shard_map(
        per_device,
        mesh=mesh,
        in_specs=placed,
        out_specs=(P("grp", "sub", None, None), P("grp", "sub", None, None)),
        check_vma=False,
    )
```
